512 devices in a mesh: dp: 16 (over x, y_lo, core), mp: 32 (over z, y_hi).
Axes of the slice: x: 4, y: 8 (y_hi: 4, y_lo: 2; y = y_hi * 2 + y_lo), z: 8, core: 2. Of those that a mesh axis runs over, the one named last changes fastest.
Arguments:
- tokens: bfloat16 [256, 4608], P('mp', 'dp'), may hold values from -6 to 6
- gate_weight: bfloat16 [4608, 36864], P('dp', 'mp'), may hold values from -0.09375 to 0.09375
- up_weight: bfloat16 [4608, 36864], P('dp', 'mp'), may hold values from -0.09375 to 0.09375
- down_weight: bfloat16 [36864, 4608], P('mp', 'dp'), may hold values from -0.03125 to 0.03125
- cotangent: bfloat16 [256, 4608], P('mp', 'dp'), may hold values from -6 to 6
Outputs:
- layer_out: float32 [256, 4608], P('mp', 'dp')
- grad_input: float32 [256, 4608], P('mp', 'dp')
- grad_gate_w: bfloat16 [4608, 36864], P('dp', 'mp')
- grad_up_w: bfloat16 [4608, 36864], P('dp', 'mp')
- grad_down_w: bfloat16 [36864, 4608], P('mp', 'dp')
The draws below stay inside these ranges and needn't reach their ends.
All inputs are finite; a program needn't handle non-finite values.
Results may differ from the reference program's by a relative error of at most 0.0049.
Values may be sent and summed in bfloat16 or wider, within the bound.
A program may use at most 64 MiB of HBM per device.

```python
import jax
import jax.numpy as jnp

D = 4608
FF = 36864
TOKENS = 256


def levels(rng, extent, pieces, low, largest):
    def one(axis_at, shards_of):
        draws = jax.random.uniform(jax.random.fold_in(jax.random.fold_in(rng, 6), axis_at), (shards_of,), jnp.float32, low / len(pieces), largest / len(pieces))
        return jnp.repeat(jnp.exp(draws), extent[axis_at] // shards_of).reshape((-1,) + (1,) * (len(extent) - axis_at - 1))

    gain = one(*pieces[0])
    for cut in pieces[1:]:
        gain = gain * one(*cut)
    return gain


def scatter_about(rng, shape, width, most, pieces=(), held_as=jnp.bfloat16):
    factor_of = levels(rng, shape, pieces, -0.22, 0.18) if pieces else 1.0
    values = jax.random.normal(rng, shape, jnp.float32) * width * factor_of
    return jnp.minimum(jnp.maximum(values, -most), most).astype(held_as)


def setup_inputs(seed: int = 0) -> dict:
    arg_keys = jax.random.split(jax.random.key(seed), 6)
    return {
        "tokens": scatter_about(arg_keys[0], (TOKENS, D), 1.0, 6.0, ((0, 32), (1, 16))),
        "gate_weight": scatter_about(arg_keys[1], (D, FF), D ** -0.5, 0.09375, ((0, 16), (1, 32))),
        "up_weight": scatter_about(arg_keys[2], (D, FF), D ** -0.5, 0.09375, ((0, 16), (1, 32))),
        "down_weight": scatter_about(arg_keys[3], (FF, D), FF ** -0.5, 0.03125, ((0, 32), (1, 16))),
        "cotangent": scatter_about(arg_keys[4], (TOKENS, D), 1.0, 6.0, ((0, 32), (1, 16))),
    }


GELU_SCALE = 0.7978845608028654
CUBIC_TERM = 0.044715


def gelu_parts(values):
    tanh_part = jnp.tanh(GELU_SCALE * (values + CUBIC_TERM * values * values * values))
    gelu_value = 0.5 * values * (1.0 + tanh_part)
    gelu_slope = 0.5 * (1.0 + tanh_part) + 0.5 * values * (1.0 - tanh_part * tanh_part) * GELU_SCALE * (1.0 + 3.0 * CUBIC_TERM * values * values)
    return gelu_value, gelu_slope


def reference(tokens, gate_weight, up_weight, down_weight, cotangent):
    gate_sums = jnp.dot(tokens, gate_weight, preferred_element_type=jnp.float32)
    up_sums = jnp.dot(tokens, up_weight, preferred_element_type=jnp.float32)
    gelu_value, gelu_slope = gelu_parts(gate_sums)
    hidden = (gelu_value * up_sums).astype(jnp.bfloat16)
    layer_out = jnp.dot(hidden, down_weight, preferred_element_type=jnp.float32)
    grad_hidden = jnp.dot(cotangent, down_weight.T, preferred_element_type=jnp.float32)
    grad_gate = (grad_hidden * up_sums * gelu_slope).astype(jnp.bfloat16)
    grad_up = (grad_hidden * gelu_value).astype(jnp.bfloat16)
    grad_down_w = jnp.dot(hidden.T, cotangent, preferred_element_type=jnp.float32).astype(jnp.bfloat16)
    grad_gate_w = jnp.dot(tokens.T, grad_gate, preferred_element_type=jnp.float32).astype(jnp.bfloat16)
    grad_up_w = jnp.dot(tokens.T, grad_up, preferred_element_type=jnp.float32).astype(jnp.bfloat16)
    grad_input = jnp.dot(grad_gate, gate_weight.T, preferred_element_type=jnp.float32) + jnp.dot(grad_up, up_weight.T, preferred_element_type=jnp.float32)
    return (layer_out, grad_input, grad_gate_w, grad_up_w, grad_down_w)
```

```python
import functools

import jax
import jax.numpy as jnp
from jax import lax
from jax.experimental import pallas as pl
from jax.experimental.pallas import tpu as pltpu
from jax.sharding import PartitionSpec as P

GELU_SCALE = 0.7978845608028654
CUBIC_TERM = 0.044715
ROWS_DIMS = (((0,), (0,)), ((), ()))
COLS_DIMS = (((1,), (1,)), ((), ()))
MESH_ID = pl.DeviceIdType.MESH
F32 = jnp.float32
BF16 = jnp.bfloat16


def gelu_parts(values):
    tanh_part = jnp.tanh(GELU_SCALE * (values + CUBIC_TERM * values * values * values))
    gelu_value = 0.5 * values * (1.0 + tanh_part)
    gelu_slope = 0.5 * (1.0 + tanh_part) + 0.5 * values * (
        1.0 - tanh_part * tanh_part
    ) * GELU_SCALE * (1.0 + 3.0 * CUBIC_TERM * values * values)
    return (gelu_value, gelu_slope)


def total_of(ref, n):
    total = ref[0].astype(F32)
    for i in range(1, n):
        total += ref[i].astype(F32)
    return total


def kernel(
    sizes,
    tok, cot, gate_h, up_h, down_h,
    lo_o, gi_o, ggw_o, guw_o, gdw_o,
    GU, DN, WB, DB, XO, XS, TK, CT, CS, PB, GB, RP, RG, HB,
    AZ, RZ, AY, RY, BY, SY, BZ, SZ, ggw_v, guw_v, gdw_v,
    ld_sem, wx_s, wx_r, p1_s, p1_r, xs_s, xs_r, rp_s, rp_r, rg_s, rg_r,
    ag_s, ag_r, fw_s, fw_r, a_s, a_r, b_s, b_r, out_sem,
):
    NQ, NZ, NY = sizes
    MP = NZ * NY
    dp = lax.axis_index("dp")
    mp = lax.axis_index("mp")
    c = lax.rem(dp, 2)
    oc = 1 - c
    q = lax.div(dp, 2)
    sib = dp + 1 - 2 * c
    z = lax.div(mp, NY)
    y = lax.rem(mp, NY)

    def rcopy(src, dst, ssem, rsem, to_dp, to_mp):
        return pltpu.make_async_remote_copy(
            src_ref=src, dst_ref=dst, send_sem=ssem, recv_sem=rsem,
            device_id=(to_dp, to_mp), device_id_type=MESH_ID,
        )

    def ahead(i, k, n):
        return lax.rem(i + k, n)

    loads = [
        pltpu.make_async_copy(gate_h, GU.at[0], ld_sem.at[0]),
        pltpu.make_async_copy(up_h, GU.at[1], ld_sem.at[1]),
        pltpu.make_async_copy(down_h, DN, ld_sem.at[2]),
    ]
    for copy in loads:
        copy.start()

    barrier = pltpu.get_barrier_semaphore()
    partners = [(sib, mp)]
    for k in range(1, NQ):
        partners.append((2 * ahead(q, k, NQ) + c, mp))
        partners.append((2 * ahead(q, k, NQ) + oc, mp))
    for k in range(1, MP):
        partners.append((dp, ahead(mp, k, MP)))
    for partner in partners:
        pl.semaphore_signal(barrier, inc=1, device_id=partner, device_id_type=MESH_ID)
    XO[mp] = jnp.concatenate([tok[...].astype(F32), cot[...].astype(F32)], axis=0).astype(BF16)
    pl.semaphore_wait(barrier, len(partners))

    p1 = []
    for k in range(1, MP):
        copy = rcopy(XO.at[mp], XO.at[mp], p1_s.at[k], p1_r.at[k], dp, ahead(mp, k, MP))
        copy.start()
        p1.append(copy)
    for copy in loads:
        copy.wait()
    wx = [
        rcopy(GU.at[oc], WB, wx_s.at[0], wx_r.at[0], sib, mp),
        rcopy(DN, DB, wx_s.at[1], wx_r.at[1], sib, mp),
    ]
    for copy in wx:
        copy.start()
    for copy in p1:
        copy.wait_recv()
    xs = rcopy(XO, XS, xs_s, xs_r, sib, mp)
    xs.start()

    def rows_of(ref):
        both = ref[...].astype(F32)
        rows, feats = both.shape[1] // 2, both.shape[2]
        both = both.reshape(MP, 2, rows, feats)
        return (
            both[:, 0].reshape(MP * rows, feats).astype(BF16),
            both[:, 1].reshape(MP * rows, feats).astype(BF16),
        )

    t_own, c_own = rows_of(XO)
    TK[...] = t_own
    CT[...] = c_own.reshape(CT.shape)
    acc = jnp.dot(t_own, GU[c], preferred_element_type=F32)
    for copy in wx:
        copy.wait_recv()
    xs.wait_recv()
    t_sib, c_sib = rows_of(XS)
    CS[...] = c_sib.reshape(CS.shape)
    acc += jnp.dot(t_sib, WB[...], preferred_element_type=F32)
    PB[...] = acc.astype(BF16).reshape(PB.shape)
    rp = []
    for k in range(NQ):
        for cc in range(2):
            if k == 0 and cc == 0:
                continue
            to = 2 * ahead(q, k, NQ) + (oc if cc else c)
            i = 2 * k + cc
            copy = rcopy(PB.at[to], RP.at[c, q], rp_s.at[i], rp_r.at[i], to, mp)
            copy.start()
            rp.append(copy)
    RP[c, q] = PB[dp]

    half = CT.shape[0] * CT.shape[2]
    feats = CT.shape[3]
    acc = lax.dot_general(
        CT[:, pl.ds(c, 1)].reshape(half, feats), DN[...], COLS_DIMS, preferred_element_type=F32
    ) + lax.dot_general(
        CS[:, pl.ds(c, 1)].reshape(half, feats), DB[...], COLS_DIMS, preferred_element_type=F32
    )
    GB[...] = acc.astype(BF16).reshape(GB.shape)
    rg = []
    for k in range(1, NQ):
        to = ahead(q, k, NQ)
        copy = rcopy(GB.at[to], RG.at[q], rg_s.at[k], rg_r.at[k], 2 * to + c, mp)
        copy.start()
        rg.append(copy)
    RG[q] = GB[q]

    for copy in rp:
        copy.wait_recv()
    g_sum = total_of(RP.at[0], NQ)
    u_sum = total_of(RP.at[1], NQ)
    gelu_value, gelu_slope = gelu_parts(g_sum)
    HB[dp, 0] = (gelu_value * u_sum).astype(BF16)
    for copy in rg:
        copy.wait_recv()
    gh_sum = total_of(RG, NQ)
    HB[dp, 1] = (gh_sum * u_sum * gelu_slope).astype(BF16)
    HB[dp, 2] = (gh_sum * gelu_value).astype(BF16)

    ag = []
    for k in range(1, NQ):
        copy = rcopy(HB.at[dp], HB.at[dp], ag_s.at[k], ag_r.at[k], 2 * ahead(q, k, NQ) + c, mp)
        copy.start()
        ag.append(copy)
    fw = [rcopy(HB.at[dp], HB.at[dp], fw_s.at[0], fw_r.at[0], sib, mp)]
    fw[0].start()
    for k in range(1, NQ):
        ag[k - 1].wait_recv()
        slot = HB.at[2 * ahead(q, NQ - k, NQ) + c]
        copy = rcopy(slot, slot, fw_s.at[k], fw_r.at[k], sib, mp)
        copy.start()
        fw.append(copy)
    for copy in fw:
        copy.wait_recv()

    tokens_n = TK.shape[0]
    units = HB.shape[3]

    def gathered(i):
        return HB[:, i].reshape(tokens_n, units)

    rows = lo_o.shape[0]
    lo = jnp.dot(gathered(0), DN[...], preferred_element_type=F32)
    AZ[...] = lo.astype(BF16).reshape(AZ.shape)
    az = []
    for k in range(1, NZ):
        to = ahead(z, k, NZ)
        copy = rcopy(AZ.at[to], RZ.at[z], a_s.at[k], a_r.at[k], dp, to * NY + y)
        copy.start()
        az.append(copy)
    RZ[z] = AZ[z]
    gi = lax.dot_general(gathered(1), GU[0], COLS_DIMS, preferred_element_type=F32)
    gi += lax.dot_general(gathered(2), GU[1], COLS_DIMS, preferred_element_type=F32)
    gi = gi.reshape(NZ, NY, rows, feats)
    for i in range(NY):
        AY[i] = gi[:, i].reshape(NZ * rows, feats).astype(BF16)
    ay = []
    for k in range(1, NY):
        to = ahead(y, k, NY)
        copy = rcopy(AY.at[to], RY.at[y], a_s.at[NZ + k], a_r.at[NZ + k], dp, z * NY + to)
        copy.start()
        ay.append(copy)
    RY[y] = AY[y]

    cts = CT[...].reshape(tokens_n, feats)
    gdw_v[...] = lax.dot_general(
        gathered(0), cts, ROWS_DIMS, preferred_element_type=F32
    ).astype(BF16)
    outs = [pltpu.make_async_copy(gdw_v, gdw_o, out_sem.at[0])]
    outs[0].start()

    for copy in az:
        copy.wait_recv()
    BY[...] = total_of(RZ, NZ).reshape(BY.shape)
    by = []
    for k in range(1, NY):
        to = ahead(y, k, NY)
        copy = rcopy(BY.at[to], SY.at[y], b_s.at[k], b_r.at[k], dp, z * NY + to)
        copy.start()
        by.append(copy)
    SY[y] = BY[y]
    for copy in ay:
        copy.wait_recv()
    BZ[...] = total_of(RY, NY).reshape(BZ.shape)
    bz = []
    for k in range(1, NZ):
        to = ahead(z, k, NZ)
        copy = rcopy(BZ.at[to], SZ.at[z], b_s.at[NY + k], b_r.at[NY + k], dp, to * NY + y)
        copy.start()
        bz.append(copy)
    SZ[z] = BZ[z]

    ggw_v[...] = lax.dot_general(
        TK[...], gathered(1), ROWS_DIMS, preferred_element_type=F32
    ).astype(BF16)
    outs.append(pltpu.make_async_copy(ggw_v, ggw_o, out_sem.at[1]))
    outs[1].start()
    guw_v[...] = lax.dot_general(
        TK[...], gathered(2), ROWS_DIMS, preferred_element_type=F32
    ).astype(BF16)
    outs.append(pltpu.make_async_copy(guw_v, guw_o, out_sem.at[2]))
    outs[2].start()

    for copy in by:
        copy.wait_recv()
    lo_o[...] = total_of(SY, NY)
    for copy in bz:
        copy.wait_recv()
    gi_o[...] = total_of(SZ, NZ)

    for copy in p1 + wx + [xs] + rp + rg + ag + fw + az + ay + by + bz:
        copy.wait_send()
    for copy in outs:
        copy.wait()


def solution(mesh):
    dp_n, mp_n = mesh.shape["dp"], mesh.shape["mp"]
    NQ, NY = dp_n // 2, min(4, mp_n // 2)
    NZ = mp_n // NY

    def local(tokens, gate_weight, up_weight, down_weight, cotangent):
        rows, F = tokens.shape
        U = gate_weight.shape[1]
        T = rows * mp_n
        R = T // dp_n
        dma = pltpu.SemaphoreType.DMA
        vmem = pl.BlockSpec(memory_space=pltpu.VMEM)
        hbm = pl.BlockSpec(memory_space=pl.ANY)
        scratch = [
            ((2, F, U), BF16), ((U, F), BF16), ((F, U), BF16), ((U, F), BF16),
            ((mp_n, 2 * rows, F), BF16), ((mp_n, 2 * rows, F), BF16),
            ((T, F), BF16), ((NQ, 2, R, F), BF16), ((NQ, 2, R, F), BF16),
            ((dp_n, R, U), BF16), ((NQ, R, U), BF16),
            ((2, NQ, R, U), BF16), ((NQ, R, U), BF16), ((dp_n, 3, R, U), BF16),
            ((NZ, NY * rows, F), BF16), ((NZ, NY * rows, F), BF16),
            ((NY, NZ * rows, F), BF16), ((NY, NZ * rows, F), BF16),
            ((NY, rows, F), F32), ((NY, rows, F), F32),
            ((NZ, rows, F), F32), ((NZ, rows, F), F32),
            ((F, U), BF16), ((F, U), BF16), ((U, F), BF16),
        ]
        sems = [3, 2, 2, mp_n, mp_n, None, None, dp_n, dp_n, NQ, NQ, NQ, NQ, NQ, NQ,
                NZ + NY, NZ + NY, NZ + NY, NZ + NY, 3]
        return pl.pallas_call(
            functools.partial(kernel, (NQ, NZ, NY)),
            out_shape=(
                jax.ShapeDtypeStruct((rows, F), F32), jax.ShapeDtypeStruct((rows, F), F32),
                jax.ShapeDtypeStruct((F, U), BF16), jax.ShapeDtypeStruct((F, U), BF16),
                jax.ShapeDtypeStruct((U, F), BF16),
            ),
            in_specs=[vmem, vmem, hbm, hbm, hbm],
            out_specs=(vmem, vmem, hbm, hbm, hbm),
            scratch_shapes=[pltpu.VMEM(s, t) for s, t in scratch]
            + [dma if n is None else dma((n,)) for n in sems],
            compiler_params=pltpu.CompilerParams(
                collective_id=0, has_side_effects=True, vmem_limit_bytes=56 * 1024 * 1024
            ),
        )(tokens, cotangent, gate_weight, up_weight, down_weight)

    return jax.shard_map(
        local,
        mesh=mesh,
        in_specs=(P("mp", "dp"), P("dp", "mp"), P("dp", "mp"), P("mp", "dp"), P("mp", "dp")),
        out_specs=(P("mp", "dp"), P("mp", "dp"), P("dp", "mp"), P("dp", "mp"), P("mp", "dp")),
        check_vma=False,
    )
```

```python
import functools

import jax
import jax.numpy as jnp
from jax import lax
from jax.experimental import pallas as pl
from jax.experimental.pallas import tpu as pltpu
from jax.sharding import PartitionSpec as P

GELU_SCALE = 0.7978845608028654
CUBIC_TERM = 0.044715
ROWS_DIMS = (((0,), (0,)), ((), ()))
COLS_DIMS = (((1,), (1,)), ((), ()))
MESH_ID = pl.DeviceIdType.MESH
F32 = jnp.float32
BF16 = jnp.bfloat16


def gelu_parts(values):
    tanh_part = jnp.tanh(GELU_SCALE * (values + CUBIC_TERM * values * values * values))
    gelu_value = 0.5 * values * (1.0 + tanh_part)
    gelu_slope = 0.5 * (1.0 + tanh_part) + 0.5 * values * (
        1.0 - tanh_part * tanh_part
    ) * GELU_SCALE * (1.0 + 3.0 * CUBIC_TERM * values * values)
    return (gelu_value, gelu_slope)


def dot(a, b):
    return jnp.dot(a, b, preferred_element_type=F32)


def dot_cols(a, b):
    return lax.dot_general(a, b, COLS_DIMS, preferred_element_type=F32)


def dot_rows(a, b):
    return lax.dot_general(a, b, ROWS_DIMS, preferred_element_type=F32)


def kernel(
    sizes,
    tok, cot, gate_h, up_h, down_h,
    lo_o, gi_o, ggw_o, guw_o, gdw_o,
    GV, UV, DV, WF, DF, WS, DS, XO, XS, TK, CT, PB, RP, HB,
    AZ, RZ, BY, SY, AF, ggw_v, guw_v, gdw_v,
    ld_sem, wx_s, wx_r, py_s, py_r, pz_s, pz_r, xs_s, xs_r, rs_s, rs_r,
    ag_s, ag_r, fw_s, fw_r, a_s, a_r, b_s, b_r, out_sem,
):
    NQ, NZ, NY = sizes
    order = [0] + [k for i in range(1, NZ // 2) for k in (i, NZ - i)] + [NZ // 2]
    slots = NZ // 2
    rows = lo_o.shape[0]
    F, H = DF.shape[1], DF.shape[2]
    part_rows = slots * NY * rows
    R = PB.shape[2]
    dp = lax.axis_index("dp")
    mp = lax.axis_index("mp")
    c = lax.rem(dp, 2)
    oc = 1 - c
    q = lax.div(dp, 2)
    sib = dp + 1 - 2 * c
    z = lax.div(mp, NY)
    y = lax.rem(mp, NY)

    sent = []

    def send(src, dst, ssem, rsem, to_dp, to_mp):
        copy = pltpu.make_async_remote_copy(
            src_ref=src, dst_ref=dst, send_sem=ssem, recv_sem=rsem,
            device_id=(to_dp, to_mp), device_id_type=MESH_ID,
        )
        copy.start()
        sent.append(copy)
        return copy

    def peer(k):
        return 2 * lax.rem(q + k, NQ) + c

    def at_z(k):
        return lax.rem(z + k, NZ) * NY + y

    def at_y(j):
        return z * NY + lax.rem(y + j, NY)

    loads = [
        pltpu.make_async_copy(gate_h, GV, ld_sem.at[0]),
        pltpu.make_async_copy(up_h, UV, ld_sem.at[1]),
        pltpu.make_async_copy(down_h, DV, ld_sem.at[2]),
    ]
    for copy in loads:
        copy.start()

    barrier = pltpu.get_barrier_semaphore()
    partners = [(sib, mp)]
    partners += [(peer(k), mp) for k in range(1, NQ)]
    partners += [(dp, at_z(k)) for k in range(1, NZ)]
    partners += [(dp, at_y(j)) for j in range(1, NY)]
    for partner in partners:
        pl.semaphore_signal(barrier, inc=1, device_id=partner, device_id_type=MESH_ID)
    XO[0, 0] = jnp.concatenate([tok[...].astype(F32), cot[...].astype(F32)], axis=0).astype(BF16)
    pl.semaphore_wait(barrier, len(partners))

    py = [
        send(XO.at[0, 0], XO.at[0, j], py_s.at[j], py_r.at[j], dp, at_y(NY - j))
        for j in range(1, NY)
    ]
    for copy in loads:
        copy.wait()
    for h in range(2):
        half = slice(h * H, (h + 1) * H)
        WF[h] = jnp.concatenate([GV[:, half], UV[:, half]], axis=1)
        DF[h] = DV[:, half]
    wx = [
        send(WF.at[oc], WS, wx_s.at[0], wx_r.at[0], sib, mp),
        send(DF.at[oc], DS, wx_s.at[1], wx_r.at[1], sib, mp),
    ]
    for copy in py:
        copy.wait_recv()
    pz = [None] + [
        send(XO.at[0], XO.at[p], pz_s.at[p], pz_r.at[p], dp, at_z(NZ - order[p]))
        for p in range(1, NZ)
    ]
    xs = [send(XO.at[0], XS.at[0], xs_s.at[0], xs_r.at[0], sib, mp)]

    def rows_of(ref, m):
        both = ref[m * slots : (m + 1) * slots].astype(F32).reshape(slots * NY, 2, rows, F)
        return (
            both[:, 0].reshape(part_rows, F).astype(BF16),
            both[:, 1].reshape(part_rows, F).astype(BF16),
        )

    rs = []
    for m in range(2):
        for p in range(max(1, m * slots), (m + 1) * slots):
            pz[p].wait_recv()
            xs.append(send(XO.at[p], XS.at[p], xs_s.at[p], xs_r.at[p], sib, mp))
        t_own, c_own = rows_of(XO, m)
        TK[m] = t_own
        CT[m] = c_own
        gu = dot(t_own, WF[c])
        gh = dot(c_own, DF[c])
        if m == 0:
            for copy in wx:
                copy.wait_recv()
        for p in range(m * slots, (m + 1) * slots):
            xs[p].wait_recv()
        t_sib, c_sib = rows_of(XS, m)
        gu += dot(t_sib, WS[...])
        PB[m, :, :, 0 : 2 * H] = gu.astype(BF16).reshape(NQ, R, 2 * H)
        gh += dot(c_sib, DS[...])
        PB[m, :, :, 2 * H : 3 * H] = gh.astype(BF16).reshape(NQ, R, H)
        rs.append([
            send(
                PB.at[m, lax.rem(q + k, NQ)], RP.at[m, q], rs_s.at[m, k], rs_r.at[m, k], peer(k), mp
            )
            for k in range(1, NQ)
        ])
        RP[m, q] = PB[m, q]

    ag = []
    fw = []
    for m in range(2):
        for copy in rs[m]:
            copy.wait_recv()
        sums = RP[m, 0].astype(F32)
        for i in range(1, NQ):
            sums += RP[m, i].astype(F32)
        g_sum, u_sum, gh_sum = sums[:, :H], sums[:, H : 2 * H], sums[:, 2 * H :]
        gelu_value, gelu_slope = gelu_parts(g_sum)
        HB[c, m, q] = jnp.concatenate(
            [gh_sum * u_sum * gelu_slope, gh_sum * gelu_value, gelu_value * u_sum], axis=1
        ).astype(BF16)
        block = HB.at[c, m, q]
        ag.append([
            send(block, block, ag_s.at[m, k], ag_r.at[m, k], peer(k), mp) for k in range(1, NQ)
        ])
        fw.append([send(block, block, fw_s.at[m, 0], fw_r.at[m, 0], sib, mp)])

    az = []
    for m in range(2):
        for k in range(1, NQ):
            ag[m][k - 1].wait_recv()
            block = HB.at[c, m, lax.rem(q + NQ - k, NQ)]
            fw[m].append(send(block, block, fw_s.at[m, k], fw_r.at[m, k], sib, mp))
        for copy in fw[m]:
            copy.wait_recv()
        acts = [HB[h, m].reshape(part_rows, 3 * H) for h in range(2)]
        lo = dot_cols(acts[0][:, 2 * H :], DF[0]) + dot_cols(acts[1][:, 2 * H :], DF[1])
        gi = dot_cols(acts[0][:, : 2 * H], WF[0]) + dot_cols(acts[1][:, : 2 * H], WF[1])
        mine = slice(m * slots, (m + 1) * slots)
        AZ[mine, 0] = lo.astype(BF16).reshape(slots, NY * rows, F)
        AZ[mine, 1] = gi.astype(BF16).reshape(slots, NY * rows, F)
        for p in range(max(1, m * slots), (m + 1) * slots):
            az.append(send(AZ.at[p], RZ.at[p], a_s.at[p], a_r.at[p], dp, at_z(order[p])))
        if m == 0:
            RZ[0] = AZ[0]

    tokens_all = TK[...].reshape(2 * part_rows, F)
    cot_all = CT[...].reshape(2 * part_rows, F)

    def full(i):
        halves = [HB[h, :, :, :, i * H : (i + 1) * H].reshape(2 * part_rows, H) for h in range(2)]
        return jnp.concatenate(halves, axis=1)

    AF[...] = full(2)
    gdw_v[...] = dot_rows(cot_all, AF[...]).astype(BF16)
    outs = [pltpu.make_async_copy(gdw_v, gdw_o, out_sem.at[0])]
    outs[0].start()

    for copy in az:
        copy.wait_recv()
    total = RZ[0].astype(F32)
    for p in range(1, NZ):
        total += RZ[p].astype(F32)
    total = total.reshape(2, NY, rows, F)
    for j in range(NY):
        BY[j] = total[:, j]
    by = [
        send(BY.at[j], SY.at[j], b_s.at[j], b_r.at[j], dp, at_y(j)) for j in range(1, NY)
    ]
    SY[0] = BY[0]

    AF[...] = full(0)
    ggw_v[...] = dot_rows(tokens_all, AF[...]).astype(BF16)
    outs.append(pltpu.make_async_copy(ggw_v, ggw_o, out_sem.at[1]))
    outs[1].start()
    AF[...] = full(1)
    guw_v[...] = dot_rows(tokens_all, AF[...]).astype(BF16)
    outs.append(pltpu.make_async_copy(guw_v, guw_o, out_sem.at[2]))
    outs[2].start()

    for copy in by:
        copy.wait_recv()
    last = SY[0]
    for j in range(1, NY):
        last += SY[j]
    lo_o[...] = last[0]
    gi_o[...] = last[1]

    for copy in sent:
        copy.wait_send()
    for copy in outs:
        copy.wait()


def copy_kernel(*refs):
    inward = [pltpu.make_async_copy(refs[i], refs[10 + i], refs[15].at[i]) for i in range(5)]
    outward = [pltpu.make_async_copy(refs[10 + i], refs[5 + i], refs[15].at[5 + i]) for i in range(5)]
    for copy in inward:
        copy.start()
    for i in range(5):
        inward[i].wait()
        outward[i].start()
    for copy in outward:
        copy.wait()


def solution(mesh):
    dp_n, mp_n = mesh.shape["dp"], mesh.shape["mp"]
    NQ, NY = dp_n // 2, min(4, mp_n // 4)
    NZ = mp_n // NY

    def local(tokens, gate_weight, up_weight, down_weight, cotangent):
        rows, F = tokens.shape
        U = gate_weight.shape[1]
        H = U // 2
        T = rows * mp_n
        R = T // dp_n
        dma = pltpu.SemaphoreType.DMA
        vmem = pl.BlockSpec(memory_space=pltpu.VMEM)
        hbm = pl.BlockSpec(memory_space=pl.ANY)
        limit = pltpu.CompilerParams(vmem_limit_bytes=60 * 1024 * 1024)
        scratch = [
            ((F, U), BF16), ((F, U), BF16), ((F, U), BF16),
            ((2, F, U), BF16), ((2, F, H), BF16), ((F, U), BF16), ((F, H), BF16),
            ((NZ, NY, 2 * rows, F), BF16), ((NZ, NY, 2 * rows, F), BF16),
            ((2, T // 2, F), BF16), ((2, T // 2, F), BF16),
            ((2, NQ, R, 3 * H), BF16), ((2, NQ, R, 3 * H), BF16), ((2, 2, NQ, R, 3 * H), BF16),
            ((NZ, 2, NY * rows, F), BF16), ((NZ, 2, NY * rows, F), BF16),
            ((NY, 2, rows, F), F32), ((NY, 2, rows, F), F32), ((T, U), BF16),
            ((F, U), BF16), ((F, U), BF16), ((F, U), BF16),
        ]
        sems = [(3,), (2,), (2,), (NY,), (NY,), (NZ,), (NZ,), (NZ,), (NZ,), (2, NQ), (2, NQ),
                (2, NQ), (2, NQ), (2, NQ), (2, NQ), (NZ,), (NZ,), (NY,), (NY,), (3,)]
        shapes = (
            jax.ShapeDtypeStruct((rows, F), F32), jax.ShapeDtypeStruct((rows, F), F32),
            jax.ShapeDtypeStruct((F, U), BF16), jax.ShapeDtypeStruct((F, U), BF16),
            jax.ShapeDtypeStruct((F, U), BF16),
        )
        results = pl.pallas_call(
            functools.partial(kernel, (NQ, NZ, NY)),
            out_shape=shapes,
            in_specs=[vmem, vmem, hbm, hbm, hbm],
            out_specs=(vmem, vmem, hbm, hbm, hbm),
            scratch_shapes=[pltpu.VMEM(s, t) for s, t in scratch] + [dma(n) for n in sems],
            compiler_params=pltpu.CompilerParams(
                collective_id=0, has_side_effects=True, vmem_limit_bytes=56 * 1024 * 1024
            ),
        )(tokens, cotangent, gate_weight, up_weight, down_weight.T)
        lo, gi, ggw, guw, gdw = pl.pallas_call(
            copy_kernel,
            out_shape=shapes,
            in_specs=[hbm] * 5,
            out_specs=(hbm,) * 5,
            scratch_shapes=[pltpu.VMEM(x.shape, x.dtype) for x in shapes] + [dma((10,))],
            compiler_params=limit,
        )(*results)
        return lo, gi, ggw, guw, gdw.T

    return jax.shard_map(
        local,
        mesh=mesh,
        in_specs=(P("mp", "dp"), P("dp", "mp"), P("dp", "mp"), P("mp", "dp"), P("mp", "dp")),
        out_specs=(P("mp", "dp"), P("mp", "dp"), P("dp", "mp"), P("dp", "mp"), P("mp", "dp")),
        check_vma=False,
    )
```

```python
import functools

import jax
import jax.numpy as jnp
from jax import lax
from jax.experimental import pallas as pl
from jax.experimental.pallas import tpu as pltpu
from jax.sharding import PartitionSpec as P

GELU_SCALE = 0.7978845608028654
CUBIC_TERM = 0.044715
ROWS_DIMS = (((0,), (0,)), ((), ()))
COLS_DIMS = (((1,), (1,)), ((), ()))
MESH_ID = pl.DeviceIdType.MESH
F32 = jnp.float32
BF16 = jnp.bfloat16


def gelu_parts(values):
    tanh_part = jnp.tanh(GELU_SCALE * (values + CUBIC_TERM * values * values * values))
    gelu_value = 0.5 * values * (1.0 + tanh_part)
    gelu_slope = 0.5 * (1.0 + tanh_part) + 0.5 * values * (
        1.0 - tanh_part * tanh_part
    ) * GELU_SCALE * (1.0 + 3.0 * CUBIC_TERM * values * values)
    return (gelu_value, gelu_slope)


def dot(a, b):
    return jnp.dot(a, b, preferred_element_type=F32)


def dot_cols(a, b):
    return lax.dot_general(a, b, COLS_DIMS, preferred_element_type=F32)


def dot_rows(a, b):
    return lax.dot_general(a, b, ROWS_DIMS, preferred_element_type=F32)


def kernel(
    sizes,
    tok_h, cot_h, gate_h, up_h, down_h,
    lo_o, gi_o, ggw_o, guw_o, gdw_o,
    tok, cot, GV, UV, DV, WF, DF, WS, DS, XO, XS, TK, CT, PB, RP, HB,
    AY, RY, AZ, RZ, BY, SY, BZ, SZ, AF, ggw_v, guw_v, gdw_v,
    ld_sem, wx_s, wx_r, py_s, py_r, pz_s, pz_r, xs_s, xs_r, rs_s, rs_r,
    ag_s, ag_r, fw_s, fw_r, ay_s, ay_r, az_s, az_r, by_s, by_r, bz_s, bz_r, out_sem,
):
    NQ, NZ, NY = sizes
    order = [0] + [k for i in range(1, NZ // 2) for k in (i, NZ - i)] + [NZ // 2]
    slots = NZ // 2
    rows = lo_o.shape[0]
    F, H = DF.shape[1], DF.shape[2]
    part_rows = slots * NY * rows
    R = PB.shape[2]
    dp = lax.axis_index("dp")
    mp = lax.axis_index("mp")
    c = lax.rem(dp, 2)
    oc = 1 - c
    q = lax.div(dp, 2)
    sib = dp + 1 - 2 * c
    z = lax.div(mp, NY)
    y = lax.rem(mp, NY)

    sent = []

    def send(src, dst, ssem, rsem, to_dp, to_mp):
        copy = pltpu.make_async_remote_copy(
            src_ref=src, dst_ref=dst, send_sem=ssem, recv_sem=rsem,
            device_id=(to_dp, to_mp), device_id_type=MESH_ID,
        )
        copy.start()
        sent.append(copy)
        return copy

    NX = NQ // 2
    qx = lax.div(q, 2)
    qy = lax.rem(q, 2)
    steps = [(dx, dy) for dx in range(NX) for dy in range(2)][1:]
    steps.sort(key=lambda s: -min(s[0], NX - s[0]) - s[1])

    def ahead(k):
        dx, dy = steps[k - 1]
        return 2 * lax.rem(qx + dx, NX) + lax.rem(qy + dy, 2)

    def behind(k):
        dx, dy = steps[k - 1]
        return 2 * lax.rem(qx + NX - dx, NX) + lax.rem(qy + dy, 2)

    def peer(k):
        return 2 * ahead(k) + c

    def at_z(k):
        return lax.rem(z + k, NZ) * NY + y

    def at_y(j):
        return z * NY + lax.rem(y + j, NY)

    loads = [
        pltpu.make_async_copy(gate_h, GV, ld_sem.at[0]),
        pltpu.make_async_copy(up_h, UV, ld_sem.at[1]),
        pltpu.make_async_copy(down_h, DV, ld_sem.at[2]),
    ]
    rows_in = [
        pltpu.make_async_copy(tok_h, tok, ld_sem.at[3]),
        pltpu.make_async_copy(cot_h, cot, ld_sem.at[4]),
    ]
    for copy in rows_in:
        copy.start()
    for copy in loads:
        copy.start()

    barrier = pltpu.get_barrier_semaphore()
    partners = [(sib, mp)]
    partners += [(peer(k), mp) for k in range(1, NQ)]
    partners += [(dp, at_z(k)) for k in range(1, NZ)]
    partners += [(dp, at_y(j)) for j in range(1, NY)]
    for partner in partners:
        pl.semaphore_signal(barrier, inc=1, device_id=partner, device_id_type=MESH_ID)
    for copy in rows_in:
        copy.wait()
    XO[0, 0] = jnp.concatenate([tok[...].astype(F32), cot[...].astype(F32)], axis=0).astype(BF16)
    pl.semaphore_wait(barrier, len(partners))

    py = [
        send(XO.at[0, 0], XO.at[0, j], py_s.at[j], py_r.at[j], dp, at_y(NY - j))
        for j in range(1, NY)
    ]
    for copy in loads:
        copy.wait()
    for h in range(2):
        half = slice(h * H, (h + 1) * H)
        WF[h] = jnp.concatenate([GV[:, half], UV[:, half]], axis=1)
        DF[h] = DV[:, half]
    wx = [
        send(WF.at[oc], WS, wx_s.at[0], wx_r.at[0], sib, mp),
        send(DF.at[oc], DS, wx_s.at[1], wx_r.at[1], sib, mp),
    ]
    for copy in py:
        copy.wait_recv()
    pz = [None] + [
        send(XO.at[0], XO.at[p], pz_s.at[p], pz_r.at[p], dp, at_z(NZ - order[p]))
        for p in range(1, NZ)
    ]
    xs = [send(XO.at[0], XS.at[0], xs_s.at[0], xs_r.at[0], sib, mp)]

    def rows_of(ref, m):
        both = ref[m * slots : (m + 1) * slots].astype(F32).reshape(slots * NY, 2, rows, F)
        return (
            both[:, 0].reshape(part_rows, F).astype(BF16),
            both[:, 1].reshape(part_rows, F).astype(BF16),
        )

    rs = []
    for m in range(2):
        for p in range(max(1, m * slots), (m + 1) * slots):
            pz[p].wait_recv()
            xs.append(send(XO.at[p], XS.at[p], xs_s.at[p], xs_r.at[p], sib, mp))
        t_own, c_own = rows_of(XO, m)
        TK[m] = t_own
        CT[m] = c_own
        gu = dot(t_own, WF[c])
        gh = dot(c_own, DF[c])
        if m == 0:
            for copy in wx:
                copy.wait_recv()
        for p in range(m * slots, (m + 1) * slots):
            xs[p].wait_recv()
        t_sib, c_sib = rows_of(XS, m)
        gu += dot(t_sib, WS[...])
        PB[m, :, :, 0 : 2 * H] = gu.astype(BF16).reshape(NQ, R, 2 * H)
        gh += dot(c_sib, DS[...])
        PB[m, :, :, 2 * H : 3 * H] = gh.astype(BF16).reshape(NQ, R, H)
        rs.append([
            send(
                PB.at[m, ahead(k)], RP.at[m, q], rs_s.at[m, k], rs_r.at[m, k], peer(k), mp
            )
            for k in range(1, NQ)
        ])
        RP[m, q] = PB[m, q]

    ag = []
    fw = []
    for m in range(2):
        for copy in rs[m]:
            copy.wait_recv()
        sums = RP[m, 0].astype(F32)
        for i in range(1, NQ):
            sums += RP[m, i].astype(F32)
        g_sum, u_sum, gh_sum = sums[:, :H], sums[:, H : 2 * H], sums[:, 2 * H :]
        gelu_value, gelu_slope = gelu_parts(g_sum)
        HB[c, m, q] = jnp.concatenate(
            [gh_sum * u_sum * gelu_slope, gh_sum * gelu_value, gelu_value * u_sum], axis=1
        ).astype(BF16)
        block = HB.at[c, m, q]
        ag.append([
            send(block, block, ag_s.at[m, k], ag_r.at[m, k], peer(k), mp) for k in range(1, NQ)
        ])
        fw.append([send(block, block, fw_s.at[m, 0], fw_r.at[m, 0], sib, mp)])

    az = []
    ay = []
    for m in range(2):
        for k in range(1, NQ):
            ag[m][k - 1].wait_recv()
            block = HB.at[c, m, behind(k)]
            fw[m].append(send(block, block, fw_s.at[m, k], fw_r.at[m, k], sib, mp))
        acts = HB[c, m].reshape(part_rows, 3 * H)
        lo = dot_cols(acts[:, 2 * H :], DF[c])
        gi = dot_cols(acts[:, : 2 * H], WF[c])
        for copy in fw[m]:
            copy.wait_recv()
        acts = HB[oc, m].reshape(part_rows, 3 * H)
        lo += dot_cols(acts[:, 2 * H :], DF[oc])
        lo = lo.reshape(slots, NY, rows, F)
        for j in range(NY):
            AY[m, j] = lo[:, j].reshape(slots * rows, F).astype(BF16)
        for j in range(1, NY):
            ay.append(send(AY.at[m, j], RY.at[m, j], ay_s.at[m, j], ay_r.at[m, j], dp, at_y(j)))
        RY[m, 0] = AY[m, 0]
        gi += dot_cols(acts[:, : 2 * H], WF[oc])
        AZ[m * slots : (m + 1) * slots] = gi.astype(BF16).reshape(slots, NY * rows, F)
        for p in range(max(1, m * slots), (m + 1) * slots):
            az.append(send(AZ.at[p], RZ.at[p], az_s.at[p], az_r.at[p], dp, at_z(order[p])))
        if m == 0:
            RZ[0] = AZ[0]

    tokens_all = TK[...].reshape(2 * part_rows, F)
    cot_all = CT[...].reshape(2 * part_rows, F)

    def full(i):
        halves = [HB[h, :, :, :, i * H : (i + 1) * H].reshape(2 * part_rows, H) for h in range(2)]
        return jnp.concatenate(halves, axis=1)

    AF[...] = full(2)
    gdw_v[...] = dot_rows(cot_all, AF[...]).astype(BF16)
    outs = [pltpu.make_async_copy(gdw_v, gdw_o, out_sem.at[0])]
    outs[0].start()

    for copy in ay:
        copy.wait_recv()
    total = RY[:, 0].astype(F32)
    for j in range(1, NY):
        total += RY[:, j].astype(F32)
    BZ[...] = total.reshape(NZ, rows, F)
    bz = [
        send(BZ.at[p], SZ.at[p], bz_s.at[p], bz_r.at[p], dp, at_z(order[p])) for p in range(1, NZ)
    ]
    for copy in az:
        copy.wait_recv()
    total = RZ[0].astype(F32)
    for p in range(1, NZ):
        total += RZ[p].astype(F32)
    BY[...] = total.reshape(NY, rows, F)
    by = [
        send(BY.at[j], SY.at[j], by_s.at[j], by_r.at[j], dp, at_y(j)) for j in range(1, NY)
    ]

    AF[...] = full(0)
    ggw_v[...] = dot_rows(tokens_all, AF[...]).astype(BF16)
    outs.append(pltpu.make_async_copy(ggw_v, ggw_o, out_sem.at[1]))
    outs[1].start()
    AF[...] = full(1)
    guw_v[...] = dot_rows(tokens_all, AF[...]).astype(BF16)
    outs.append(pltpu.make_async_copy(guw_v, guw_o, out_sem.at[2]))
    outs[2].start()

    for copy in by:
        copy.wait_recv()
    last = BY[0]
    for j in range(1, NY):
        last += SY[j]
    gi_o[...] = last
    for copy in bz:
        copy.wait_recv()
    last = BZ[0]
    for p in range(1, NZ):
        last += SZ[p]
    lo_o[...] = last

    for copy in sent:
        copy.wait_send()
    for copy in outs:
        copy.wait()


def copy_kernel(*refs):
    inward = [pltpu.make_async_copy(refs[i], refs[10 + i], refs[15].at[0, i]) for i in range(5)]
    outward = [pltpu.make_async_copy(refs[10 + i], refs[5 + i], refs[15].at[1, i]) for i in range(5)]
    for copy in inward:
        copy.start()
    for come, go in zip(inward, outward):
        come.wait()
        go.start()
    for copy in outward:
        copy.wait()


def solution(mesh):
    dp_n, mp_n = mesh.shape["dp"], mesh.shape["mp"]
    NQ, NY = dp_n // 2, min(4, mp_n // 4)
    NZ = mp_n // NY

    def local(tokens, gate_weight, up_weight, down_weight, cotangent):
        rows, F = tokens.shape
        U = gate_weight.shape[1]
        H = U // 2
        T = rows * mp_n
        R = T // dp_n
        dma = pltpu.SemaphoreType.DMA
        vmem = pl.BlockSpec(memory_space=pltpu.VMEM)
        hbm = pl.BlockSpec(memory_space=pltpu.HBM)
        anywhere = pl.BlockSpec(memory_space=pl.ANY)
        limit = pltpu.CompilerParams(vmem_limit_bytes=60 * 1024 * 1024)
        scratch = [
            ((rows, F), BF16), ((rows, F), BF16),
            ((F, U), BF16), ((F, U), BF16), ((F, U), BF16),
            ((2, F, U), BF16), ((2, F, H), BF16), ((F, U), BF16), ((F, H), BF16),
            ((NZ, NY, 2 * rows, F), BF16), ((NZ, NY, 2 * rows, F), BF16),
            ((2, T // 2, F), BF16), ((2, T // 2, F), BF16),
            ((2, NQ, R, 3 * H), BF16), ((2, NQ, R, 3 * H), BF16), ((2, 2, NQ, R, 3 * H), BF16),
            ((2, NY, NZ // 2 * rows, F), BF16), ((2, NY, NZ // 2 * rows, F), BF16),
            ((NZ, NY * rows, F), BF16), ((NZ, NY * rows, F), BF16),
            ((NY, rows, F), F32), ((NY, rows, F), F32),
            ((NZ, rows, F), F32), ((NZ, rows, F), F32), ((T, U), BF16),
            ((F, U), BF16), ((F, U), BF16), ((F, U), BF16),
        ]
        sems = [(5,), (2,), (2,), (NY,), (NY,), (NZ,), (NZ,), (NZ,), (NZ,), (2, NQ), (2, NQ),
                (2, NQ), (2, NQ), (2, NQ), (2, NQ), (2, NY), (2, NY), (NZ,), (NZ,),
                (NY,), (NY,), (NZ,), (NZ,), (3,)]
        shapes = (
            jax.ShapeDtypeStruct((rows, F), F32), jax.ShapeDtypeStruct((rows, F), F32),
            jax.ShapeDtypeStruct((F, U), BF16), jax.ShapeDtypeStruct((F, U), BF16),
            jax.ShapeDtypeStruct((F, U), BF16),
        )
        results = pl.pallas_call(
            functools.partial(kernel, (NQ, NZ, NY)),
            out_shape=shapes,
            in_specs=[hbm] * 5,
            out_specs=(vmem, vmem, anywhere, anywhere, anywhere),
            scratch_shapes=[pltpu.VMEM(s, t) for s, t in scratch] + [dma(n) for n in sems],
            compiler_params=pltpu.CompilerParams(
                collective_id=0, has_side_effects=True, vmem_limit_bytes=56 * 1024 * 1024
            ),
        )(tokens, cotangent, gate_weight, up_weight, down_weight.T)
        lo, gi, ggw, guw, gdw = pl.pallas_call(
            copy_kernel,
            out_shape=shapes,
            in_specs=[anywhere] * 5,
            out_specs=(anywhere,) * 5,
            scratch_shapes=[pltpu.VMEM(x.shape, x.dtype) for x in shapes] + [dma((2, 5))],
            compiler_params=limit,
        )(*results)
        return lo, gi, ggw, guw, gdw.T

    return jax.shard_map(
        local,
        mesh=mesh,
        in_specs=(P("mp", "dp"), P("dp", "mp"), P("dp", "mp"), P("mp", "dp"), P("mp", "dp")),
        out_specs=(P("mp", "dp"), P("mp", "dp"), P("dp", "mp"), P("dp", "mp"), P("mp", "dp")),
        check_vma=False,
    )
```

```python
import functools

import jax
import jax.numpy as jnp
from jax import lax
from jax.experimental import pallas as pl
from jax.experimental.pallas import tpu as pltpu
from jax.sharding import PartitionSpec as P

GELU_SCALE = 0.7978845608028654
CUBIC_TERM = 0.044715
ROWS_DIMS = (((0,), (0,)), ((), ()))
COLS_DIMS = (((1,), (1,)), ((), ()))
MESH_ID = pl.DeviceIdType.MESH
F32 = jnp.float32
BF16 = jnp.bfloat16
LANES = 128


def gelu_parts(values):
    tanh_part = jnp.tanh(GELU_SCALE * (values + CUBIC_TERM * values * values * values))
    gelu_value = 0.5 * values * (1.0 + tanh_part)
    gelu_slope = 0.5 * (1.0 + tanh_part) + 0.5 * values * (
        1.0 - tanh_part * tanh_part
    ) * GELU_SCALE * (1.0 + 3.0 * CUBIC_TERM * values * values)
    return (gelu_value, gelu_slope)


def dot(a, b):
    return jnp.dot(a, b, preferred_element_type=F32)


def dot_cols(a, b):
    return lax.dot_general(a, b, COLS_DIMS, preferred_element_type=F32)


def dot_rows(a, b):
    return lax.dot_general(a, b, ROWS_DIMS, preferred_element_type=F32)


def kernel(
    sizes,
    tok_h, cot_h, gate_h, up_h, down_h,
    lo_o, gi_o, ggw_o, guw_o, gdw_o,
    tok, cot, GV, UV, DV, WF, DF, WS, DS, XY, XO, XS, TK, CT, PB, RP, HB,
    AY, RY, AZ, RZ, BY, SY, BZ, SZ, AF, ggw_v, guw_v, gdw_v,
    ld_sem, wx_s, wx_r, py_s, py_r, pz_s, pz_r, xs_s, xs_r, rs_s, rs_r,
    ag_s, ag_r, fw_s, fw_r, ay_s, ay_r, az_s, az_r, by_s, by_r, bz_s, bz_r, out_sem,
):
    NQ, NZ, NY = sizes
    order = [0]
    for first in (2, 1):
        order += sorted(range(first, NZ, 2), key=lambda k: -min(k, NZ - k))
    slots = NZ // 2
    rows = lo_o.shape[0]
    F, H = DF.shape[1], DF.shape[2]
    part_rows = slots * NY * rows
    R = PB.shape[2]
    dp = lax.axis_index("dp")
    mp = lax.axis_index("mp")
    c = lax.rem(dp, 2)
    oc = 1 - c
    q = lax.div(dp, 2)
    sib = dp + 1 - 2 * c
    z = lax.div(mp, NY)
    y = lax.rem(mp, NY)

    sent = []

    def send(src, dst, ssem, rsem, to_dp, to_mp):
        copy = pltpu.make_async_remote_copy(
            src_ref=src, dst_ref=dst, send_sem=ssem, recv_sem=rsem,
            device_id=(to_dp, to_mp), device_id_type=MESH_ID,
        )
        copy.start()
        sent.append(copy)
        return copy

    NX = NQ // 2
    qx = lax.div(q, 2)
    qy = lax.rem(q, 2)
    steps = [(dx, dy) for dx in range(NX) for dy in range(2)][1:]
    steps.sort(key=lambda s: -min(s[0], NX - s[0]) - s[1])

    def ahead(k):
        dx, dy = steps[k - 1]
        return 2 * lax.rem(qx + dx, NX) + lax.rem(qy + dy, 2)

    def behind(k):
        dx, dy = steps[k - 1]
        return 2 * lax.rem(qx + NX - dx, NX) + lax.rem(qy + dy, 2)

    def peer(k):
        return 2 * ahead(k) + c

    def at_z(k):
        return lax.rem(z + k, NZ) * NY + y

    def at_y(j):
        return z * NY + lax.rem(y + j, NY)

    loads = [
        pltpu.make_async_copy(gate_h, GV, ld_sem.at[0]),
        pltpu.make_async_copy(up_h, UV, ld_sem.at[1]),
        pltpu.make_async_copy(down_h, DV, ld_sem.at[2]),
    ]
    rows_in = [
        pltpu.make_async_copy(tok_h, tok, ld_sem.at[3]),
        pltpu.make_async_copy(cot_h, cot, ld_sem.at[4]),
    ]
    for copy in rows_in:
        copy.start()
    for copy in loads:
        copy.start()

    barrier = pltpu.get_barrier_semaphore()
    partners = [(sib, mp)]
    partners += [(peer(k), mp) for k in range(1, NQ)]
    partners += [(dp, at_z(k)) for k in range(1, NZ)]
    partners += [(dp, at_y(j)) for j in range(1, NY)]
    for partner in partners:
        pl.semaphore_signal(barrier, inc=1, device_id=partner, device_id_type=MESH_ID)
    for copy in rows_in:
        copy.wait()
    XY[0] = jnp.concatenate([tok[...].astype(F32), cot[...].astype(F32)], axis=0).astype(BF16)
    pl.semaphore_wait(barrier, len(partners))

    py = [
        send(XY.at[0], XY.at[j], py_s.at[j], py_r.at[j], dp, at_y(NY - j))
        for j in sorted(range(1, NY), key=lambda j: -min(j, NY - j))
    ]
    for copy in loads:
        copy.wait()
    for h in range(2):
        half = slice(h * H, (h + 1) * H)
        WF[h] = jnp.concatenate([GV[:, half], UV[:, half]], axis=1)
        DF[h] = DV[:, half]
    wx = [
        send(WF.at[oc], WS, wx_s.at[0], wx_r.at[0], sib, mp),
        send(DF.at[oc], DS, wx_s.at[1], wx_r.at[1], sib, mp),
    ]
    for copy in py:
        copy.wait_recv()
    lanes = XO.shape[2]
    whole, rest = F // lanes, F % lanes
    block_rows = NY * 2 * rows
    for t in range(whole):
        XO[0, t * block_rows : (t + 1) * block_rows] = XY[
            :, :, t * lanes : (t + 1) * lanes
        ].reshape(block_rows, lanes)
    if rest:
        XO[0, whole * block_rows :] = jnp.concatenate(
            [XY[j, :, whole * lanes :] for j in range(NY)], axis=1
        )
    pz = [None] + [
        send(XO.at[0], XO.at[p], pz_s.at[p], pz_r.at[p], dp, at_z(NZ - order[p]))
        for p in range(1, NZ)
    ]
    xs = [send(XO.at[0], XS.at[0], xs_s.at[0], xs_r.at[0], sib, mp)]

    def rows_of(ref, m):
        packed = ref[m * slots : (m + 1) * slots].astype(F32)
        both = [packed[:, t * block_rows : (t + 1) * block_rows] for t in range(whole)]
        if rest:
            last = packed[:, whole * block_rows :]
            last = [last[:, :, j * rest : (j + 1) * rest] for j in range(NY)]
            both.append(jnp.stack(last, axis=1).reshape(slots, block_rows, rest))
        both = jnp.concatenate(both, axis=2).reshape(slots * NY, 2, rows, F)
        return (
            both[:, 0].reshape(part_rows, F).astype(BF16),
            both[:, 1].reshape(part_rows, F).astype(BF16),
        )

    rs = []
    for m in range(2):
        for p in range(max(1, m * slots), (m + 1) * slots):
            pz[p].wait_recv()
            xs.append(send(XO.at[p], XS.at[p], xs_s.at[p], xs_r.at[p], sib, mp))
        t_own, c_own = rows_of(XO, m)
        TK[m] = t_own
        CT[m] = c_own
        gu = dot(t_own, WF[c])
        gh = dot(c_own, DF[c])
        if m == 0:
            for copy in wx:
                copy.wait_recv()
        for p in range(m * slots, (m + 1) * slots):
            xs[p].wait_recv()
        t_sib, c_sib = rows_of(XS, m)
        gu += dot(t_sib, WS[...])
        PB[m, :, :, 0 : 2 * H] = gu.astype(BF16).reshape(NQ, R, 2 * H)
        gh += dot(c_sib, DS[...])
        PB[m, :, :, 2 * H : 3 * H] = gh.astype(BF16).reshape(NQ, R, H)
        rs.append([
            send(
                PB.at[m, ahead(k)], RP.at[m, q], rs_s.at[m, k], rs_r.at[m, k], peer(k), mp
            )
            for k in range(1, NQ)
        ])
        RP[m, q] = PB[m, q]

    ag = []
    fw = []
    for m in range(2):
        for copy in rs[m]:
            copy.wait_recv()
        sums = RP[m, 0].astype(F32)
        for i in range(1, NQ):
            sums += RP[m, i].astype(F32)
        g_sum, u_sum, gh_sum = sums[:, :H], sums[:, H : 2 * H], sums[:, 2 * H :]
        gelu_value, gelu_slope = gelu_parts(g_sum)
        HB[c, m, q] = jnp.concatenate(
            [gh_sum * u_sum * gelu_slope, gh_sum * gelu_value, gelu_value * u_sum], axis=1
        ).astype(BF16)
        block = HB.at[c, m, q]
        ag.append([
            send(block, block, ag_s.at[m, k], ag_r.at[m, k], peer(k), mp) for k in range(1, NQ)
        ])
        fw.append([send(block, block, fw_s.at[m, 0], fw_r.at[m, 0], sib, mp)])

    az = []
    ay = []
    for m in range(2):
        for k in range(NQ - 1, 0, -1):
            ag[m][k - 1].wait_recv()
            block = HB.at[c, m, behind(k)]
            fw[m].append(send(block, block, fw_s.at[m, k], fw_r.at[m, k], sib, mp))
        acts = HB[c, m].reshape(part_rows, 3 * H)
        lo = dot_cols(acts[:, 2 * H :], DF[c])
        gi = dot_cols(acts[:, : 2 * H], WF[c])
        for copy in fw[m]:
            copy.wait_recv()
        acts = HB[oc, m].reshape(part_rows, 3 * H)
        lo += dot_cols(acts[:, 2 * H :], DF[oc])
        lo = lo.reshape(slots, NY, rows, F)
        for j in range(NY):
            AY[m, j] = lo[:, j].reshape(slots * rows, F).astype(BF16)
        for j in range(1, NY):
            ay.append(send(AY.at[m, j], RY.at[m, j], ay_s.at[m, j], ay_r.at[m, j], dp, at_y(j)))
        RY[m, 0] = AY[m, 0]
        gi += dot_cols(acts[:, : 2 * H], WF[oc])
        AZ[m * slots : (m + 1) * slots] = gi.astype(BF16).reshape(slots, NY * rows, F)
        for p in range(max(1, m * slots), (m + 1) * slots):
            az.append(send(AZ.at[p], RZ.at[p], az_s.at[p], az_r.at[p], dp, at_z(order[p])))
        if m == 0:
            RZ[0] = AZ[0]

    tokens_all = TK[...].reshape(2 * part_rows, F)
    cot_all = CT[...].reshape(2 * part_rows, F)

    def full(i):
        halves = [HB[h, :, :, :, i * H : (i + 1) * H].reshape(2 * part_rows, H) for h in range(2)]
        return jnp.concatenate(halves, axis=1)

    AF[...] = full(2)
    gdw_v[...] = dot_rows(cot_all, AF[...]).astype(BF16)
    outs = [pltpu.make_async_copy(gdw_v, gdw_o, out_sem.at[0])]
    outs[0].start()

    for copy in ay:
        copy.wait_recv()
    total = RY[:, 0].astype(F32)
    for j in range(1, NY):
        total += RY[:, j].astype(F32)
    BZ[...] = total.reshape(NZ, rows, F)
    bz = [
        send(BZ.at[p], SZ.at[p], bz_s.at[p], bz_r.at[p], dp, at_z(order[p])) for p in range(1, NZ)
    ]
    for copy in az:
        copy.wait_recv()
    total = RZ[0].astype(F32)
    for p in range(1, NZ):
        total += RZ[p].astype(F32)
    BY[...] = total.reshape(NY, rows, F)
    by = [
        send(BY.at[j], SY.at[j], by_s.at[j], by_r.at[j], dp, at_y(j)) for j in range(1, NY)
    ]

    AF[...] = full(0)
    ggw_v[...] = dot_rows(tokens_all, AF[...]).astype(BF16)
    outs.append(pltpu.make_async_copy(ggw_v, ggw_o, out_sem.at[1]))
    outs[1].start()
    AF[...] = full(1)
    guw_v[...] = dot_rows(tokens_all, AF[...]).astype(BF16)
    outs.append(pltpu.make_async_copy(guw_v, guw_o, out_sem.at[2]))
    outs[2].start()

    for copy in by:
        copy.wait_recv()
    last = BY[0]
    for j in range(1, NY):
        last += SY[j]
    gi_o[...] = last
    for copy in bz:
        copy.wait_recv()
    last = BZ[0]
    for p in range(1, NZ):
        last += SZ[p]
    lo_o[...] = last

    for copy in sent:
        copy.wait_send()
    for copy in outs:
        copy.wait()


def copy_kernel(*refs):
    inward = [pltpu.make_async_copy(refs[i], refs[10 + i], refs[15].at[0, i]) for i in range(5)]
    outward = [pltpu.make_async_copy(refs[10 + i], refs[5 + i], refs[15].at[1, i]) for i in range(5)]
    for copy in inward:
        copy.start()
    for come, go in zip(inward, outward):
        come.wait()
        go.start()
    for copy in outward:
        copy.wait()


def solution(mesh):
    dp_n, mp_n = mesh.shape["dp"], mesh.shape["mp"]
    NQ, NY = dp_n // 2, min(4, mp_n // 4)
    NZ = mp_n // NY

    def local(tokens, gate_weight, up_weight, down_weight, cotangent):
        rows, F = tokens.shape
        U = gate_weight.shape[1]
        H = U // 2
        packed = F // LANES * NY * 2 * rows + (2 * rows if F % LANES else 0)
        T = rows * mp_n
        R = T // dp_n
        dma = pltpu.SemaphoreType.DMA
        vmem = pl.BlockSpec(memory_space=pltpu.VMEM)
        hbm = pl.BlockSpec(memory_space=pltpu.HBM)
        anywhere = pl.BlockSpec(memory_space=pl.ANY)
        limit = pltpu.CompilerParams(vmem_limit_bytes=60 * 1024 * 1024)
        scratch = [
            ((rows, F), BF16), ((rows, F), BF16),
            ((F, U), BF16), ((F, U), BF16), ((F, U), BF16),
            ((2, F, U), BF16), ((2, F, H), BF16), ((F, U), BF16), ((F, H), BF16),
            ((NY, 2 * rows, F), BF16), ((NZ, packed, LANES), BF16), ((NZ, packed, LANES), BF16),
            ((2, T // 2, F), BF16), ((2, T // 2, F), BF16),
            ((2, NQ, R, 3 * H), BF16), ((2, NQ, R, 3 * H), BF16), ((2, 2, NQ, R, 3 * H), BF16),
            ((2, NY, NZ // 2 * rows, F), BF16), ((2, NY, NZ // 2 * rows, F), BF16),
            ((NZ, NY * rows, F), BF16), ((NZ, NY * rows, F), BF16),
            ((NY, rows, F), F32), ((NY, rows, F), F32),
            ((NZ, rows, F), F32), ((NZ, rows, F), F32), ((T, U), BF16),
            ((F, U), BF16), ((F, U), BF16), ((F, U), BF16),
        ]
        sems = [(5,), (2,), (2,), (NY,), (NY,), (NZ,), (NZ,), (NZ,), (NZ,), (2, NQ), (2, NQ),
                (2, NQ), (2, NQ), (2, NQ), (2, NQ), (2, NY), (2, NY), (NZ,), (NZ,),
                (NY,), (NY,), (NZ,), (NZ,), (3,)]
        shapes = (
            jax.ShapeDtypeStruct((rows, F), F32), jax.ShapeDtypeStruct((rows, F), F32),
            jax.ShapeDtypeStruct((F, U), BF16), jax.ShapeDtypeStruct((F, U), BF16),
            jax.ShapeDtypeStruct((F, U), BF16),
        )
        results = pl.pallas_call(
            functools.partial(kernel, (NQ, NZ, NY)),
            out_shape=shapes,
            in_specs=[hbm] * 5,
            out_specs=(vmem, vmem, anywhere, anywhere, anywhere),
            scratch_shapes=[pltpu.VMEM(s, t) for s, t in scratch] + [dma(n) for n in sems],
            compiler_params=pltpu.CompilerParams(
                collective_id=0, has_side_effects=True, vmem_limit_bytes=56 * 1024 * 1024
            ),
        )(tokens, cotangent, gate_weight, up_weight, down_weight.T)
        lo, gi, ggw, guw, gdw = pl.pallas_call(
            copy_kernel,
            out_shape=shapes,
            in_specs=[anywhere] * 5,
            out_specs=(anywhere,) * 5,
            scratch_shapes=[pltpu.VMEM(x.shape, x.dtype) for x in shapes] + [dma((2, 5))],
            compiler_params=limit,
        )(*results)
        return lo, gi, ggw, guw, gdw.T

    return jax.shard_map(
        local,
        mesh=mesh,
        in_specs=(P("mp", "dp"), P("dp", "mp"), P("dp", "mp"), P("mp", "dp"), P("mp", "dp")),
        out_specs=(P("mp", "dp"), P("mp", "dp"), P("dp", "mp"), P("dp", "mp"), P("mp", "dp")),
        check_vma=False,
    )
```

```python
import functools

import jax
import jax.numpy as jnp
from jax import lax
from jax.experimental import pallas as pl
from jax.experimental.pallas import tpu as pltpu
from jax.sharding import PartitionSpec as P

GELU_SCALE = 0.7978845608028654
CUBIC_TERM = 0.044715
ROWS_DIMS = (((0,), (0,)), ((), ()))
COLS_DIMS = (((1,), (1,)), ((), ()))
MESH_ID = pl.DeviceIdType.MESH
F32 = jnp.float32
BF16 = jnp.bfloat16
LANES = 128


def gelu_parts(values):
    tanh_part = jnp.tanh(GELU_SCALE * (values + CUBIC_TERM * values * values * values))
    gelu_value = 0.5 * values * (1.0 + tanh_part)
    gelu_slope = 0.5 * (1.0 + tanh_part) + 0.5 * values * (
        1.0 - tanh_part * tanh_part
    ) * GELU_SCALE * (1.0 + 3.0 * CUBIC_TERM * values * values)
    return (gelu_value, gelu_slope)


def dot(a, b):
    return jnp.dot(a, b, preferred_element_type=F32)


def dot_cols(a, b):
    return lax.dot_general(a, b, COLS_DIMS, preferred_element_type=F32)


def dot_rows(a, b):
    return lax.dot_general(a, b, ROWS_DIMS, preferred_element_type=F32)


def kernel(
    sizes,
    tok_h, cot_h, gate_h, up_h, down_h,
    SZ, SY, ggw_o, guw_o, gdw_o,
    tok, cot, GV, UV, DV, WF, DF, WS, DS, XY, XO, XS, TK, CT, PB, RP, HB,
    AY, RY, AZ, RZ, BY, BZ, AF, ggw_v, guw_v, gdw_v,
    ld_sem, wx_s, wx_r, py_s, py_r, pz_s, pz_r, xs_s, xs_r, rs_s, rs_r,
    ag_s, ag_r, fw_s, fw_r, ay_s, ay_r, az_s, az_r, by_s, by_r, bz_s, bz_r, out_sem,
):
    NQ, NZ, NY = sizes
    order = [0]
    for first in (2, 1):
        order += sorted(range(first, NZ, 2), key=lambda k: -min(k, NZ - k))
    slots = NZ // 2
    rows = tok.shape[0]
    F, H = DF.shape[1], DF.shape[2]
    part_rows = slots * NY * rows
    R = PB.shape[2]
    dp = lax.axis_index("dp")
    mp = lax.axis_index("mp")
    c = lax.rem(dp, 2)
    oc = 1 - c
    q = lax.div(dp, 2)
    sib = dp + 1 - 2 * c
    z = lax.div(mp, NY)
    y = lax.rem(mp, NY)

    sent = []

    def send(src, dst, ssem, rsem, to_dp, to_mp):
        copy = pltpu.make_async_remote_copy(
            src_ref=src, dst_ref=dst, send_sem=ssem, recv_sem=rsem,
            device_id=(to_dp, to_mp), device_id_type=MESH_ID,
        )
        copy.start()
        sent.append(copy)
        return copy

    def drain(n):
        for copy in sent[:n]:
            copy.wait_send()
        del sent[:n]

    NX = NQ // 2
    qx = lax.div(q, 2)
    qy = lax.rem(q, 2)
    steps = [(dx, dy) for dx in range(NX) for dy in range(2)][1:]
    steps.sort(key=lambda s: -min(s[0], NX - s[0]) - s[1])

    def ahead(k):
        dx, dy = steps[k - 1]
        return 2 * lax.rem(qx + dx, NX) + lax.rem(qy + dy, 2)

    def behind(k):
        dx, dy = steps[k - 1]
        return 2 * lax.rem(qx + NX - dx, NX) + lax.rem(qy + dy, 2)

    def peer(k):
        return 2 * ahead(k) + c

    def at_z(k):
        return lax.rem(z + k, NZ) * NY + y

    def at_y(j):
        return z * NY + lax.rem(y + j, NY)

    loads = [
        pltpu.make_async_copy(gate_h, GV, ld_sem.at[0]),
        pltpu.make_async_copy(up_h, UV, ld_sem.at[1]),
        pltpu.make_async_copy(down_h, DV, ld_sem.at[2]),
    ]
    rows_in = [
        pltpu.make_async_copy(tok_h, tok, ld_sem.at[3]),
        pltpu.make_async_copy(cot_h, cot, ld_sem.at[4]),
    ]
    for copy in rows_in:
        copy.start()
    for copy in loads:
        copy.start()

    barrier = pltpu.get_barrier_semaphore()
    partners = [(sib, mp)]
    partners += [(peer(k), mp) for k in range(1, NQ)]
    partners += [(dp, at_z(k)) for k in range(1, NZ)]
    partners += [(dp, at_y(j)) for j in range(1, NY)]
    for partner in partners:
        pl.semaphore_signal(barrier, inc=1, device_id=partner, device_id_type=MESH_ID)
    for copy in rows_in:
        copy.wait()
    XY[0] = jnp.concatenate([tok[...].astype(F32), cot[...].astype(F32)], axis=0).astype(BF16)
    pl.semaphore_wait(barrier, len(partners))

    py = [
        send(XY.at[0], XY.at[j], py_s.at[j], py_r.at[j], dp, at_y(NY - j))
        for j in sorted(range(1, NY), key=lambda j: -min(j, NY - j))
    ]
    for copy in loads:
        copy.wait()
    for h in range(2):
        half = slice(h * H, (h + 1) * H)
        WF[h] = jnp.concatenate([GV[:, half], UV[:, half]], axis=1)
        DF[h] = DV[:, half]
    wx = [
        send(WF.at[oc], WS, wx_s.at[0], wx_r.at[0], sib, mp),
        send(DF.at[oc], DS, wx_s.at[1], wx_r.at[1], sib, mp),
    ]
    for copy in py:
        copy.wait_recv()
    lanes = XO.shape[2]
    whole, rest = F // lanes, F % lanes
    block_rows = NY * 2 * rows
    for t in range(whole):
        XO[0, t * block_rows : (t + 1) * block_rows] = XY[
            :, :, t * lanes : (t + 1) * lanes
        ].reshape(block_rows, lanes)
    if rest:
        XO[0, whole * block_rows :] = jnp.concatenate(
            [XY[j, :, whole * lanes :] for j in range(NY)], axis=1
        )
    pz = [None] + [
        send(XO.at[0], XO.at[p], pz_s.at[p], pz_r.at[p], dp, at_z(NZ - order[p]))
        for p in range(1, NZ)
    ]
    xs = [send(XO.at[0], XS.at[0], xs_s.at[0], xs_r.at[0], sib, mp)]

    def rows_of(ref, m):
        packed = ref[m * slots : (m + 1) * slots].astype(F32)
        both = [packed[:, t * block_rows : (t + 1) * block_rows] for t in range(whole)]
        if rest:
            last = packed[:, whole * block_rows :]
            last = [last[:, :, j * rest : (j + 1) * rest] for j in range(NY)]
            both.append(jnp.stack(last, axis=1).reshape(slots, block_rows, rest))
        both = jnp.concatenate(both, axis=2).reshape(slots * NY, 2, rows, F)
        return (
            both[:, 0].reshape(part_rows, F).astype(BF16),
            both[:, 1].reshape(part_rows, F).astype(BF16),
        )

    rs = []
    for m in range(2):
        for p in range(max(1, m * slots), (m + 1) * slots):
            pz[p].wait_recv()
            xs.append(send(XO.at[p], XS.at[p], xs_s.at[p], xs_r.at[p], sib, mp))
        t_own, c_own = rows_of(XO, m)
        TK[m] = t_own
        CT[m] = c_own
        gu = dot(t_own, WF[c])
        gh = dot(c_own, DF[c])
        if m == 0:
            for copy in wx:
                copy.wait_recv()
        for p in range(m * slots, (m + 1) * slots):
            xs[p].wait_recv()
        t_sib, c_sib = rows_of(XS, m)
        gu += dot(t_sib, WS[...])
        PB[m, :, :, 0 : 2 * H] = gu.astype(BF16).reshape(NQ, R, 2 * H)
        gh += dot(c_sib, DS[...])
        PB[m, :, :, 2 * H : 3 * H] = gh.astype(BF16).reshape(NQ, R, H)
        rs.append([
            send(
                PB.at[m, ahead(k)], RP.at[m, q], rs_s.at[m, k], rs_r.at[m, k], peer(k), mp
            )
            for k in range(1, NQ)
        ])
        RP[m, q] = PB[m, q]

    ag = []
    fw = []
    for m in range(2):
        for copy in rs[m]:
            copy.wait_recv()
        sums = RP[m, 0].astype(F32)
        for i in range(1, NQ):
            sums += RP[m, i].astype(F32)
        g_sum, u_sum, gh_sum = sums[:, :H], sums[:, H : 2 * H], sums[:, 2 * H :]
        gelu_value, gelu_slope = gelu_parts(g_sum)
        HB[c, m, q] = jnp.concatenate(
            [gh_sum * u_sum * gelu_slope, gh_sum * gelu_value, gelu_value * u_sum], axis=1
        ).astype(BF16)
        block = HB.at[c, m, q]
        ag.append([
            send(block, block, ag_s.at[m, k], ag_r.at[m, k], peer(k), mp) for k in range(1, NQ)
        ])
        fw.append([send(block, block, fw_s.at[m, 0], fw_r.at[m, 0], sib, mp)])

    az = []
    ay = []
    for m in range(2):
        for k in range(NQ - 1, 0, -1):
            ag[m][k - 1].wait_recv()
            block = HB.at[c, m, behind(k)]
            fw[m].append(send(block, block, fw_s.at[m, k], fw_r.at[m, k], sib, mp))
        acts = HB[c, m].reshape(part_rows, 3 * H)
        lo = dot_cols(acts[:, 2 * H :], DF[c])
        gi = dot_cols(acts[:, : 2 * H], WF[c])
        for copy in fw[m]:
            copy.wait_recv()
        acts = HB[oc, m].reshape(part_rows, 3 * H)
        lo += dot_cols(acts[:, 2 * H :], DF[oc])
        lo = lo.reshape(slots, NY, rows, F)
        for j in range(NY):
            AY[m, j] = lo[:, j].reshape(slots * rows, F).astype(BF16)
        for j in range(1, NY):
            ay.append(send(AY.at[m, j], RY.at[m, j], ay_s.at[m, j], ay_r.at[m, j], dp, at_y(j)))
        RY[m, 0] = AY[m, 0]
        gi += dot_cols(acts[:, : 2 * H], WF[oc])
        AZ[m * slots : (m + 1) * slots] = gi.astype(BF16).reshape(slots, NY * rows, F)
        for p in range(max(1, m * slots), (m + 1) * slots):
            az.append(send(AZ.at[p], RZ.at[p], az_s.at[p], az_r.at[p], dp, at_z(order[p])))
        if m == 0:
            RZ[0] = AZ[0]

    tokens_all = TK[...].reshape(2 * part_rows, F)
    cot_all = CT[...].reshape(2 * part_rows, F)

    def full(i):
        halves = [HB[h, :, :, :, i * H : (i + 1) * H].reshape(2 * part_rows, H) for h in range(2)]
        return jnp.concatenate(halves, axis=1)

    AF[...] = full(2)
    gdw_v[...] = dot_rows(cot_all, AF[...]).astype(BF16)
    outs = [pltpu.make_async_copy(gdw_v, gdw_o, out_sem.at[0])]
    outs[0].start()

    for copy in ay:
        copy.wait_recv()
    total = RY[:, 0].astype(F32)
    for j in range(1, NY):
        total += RY[:, j].astype(F32)
    BZ[...] = total.reshape(NZ, rows, F)
    bz = [
        send(BZ.at[p], SZ.at[p], bz_s.at[p], bz_r.at[p], dp, at_z(order[p])) for p in range(1, NZ)
    ]
    for copy in az:
        copy.wait_recv()
    total = RZ[0].astype(F32)
    for p in range(1, NZ):
        total += RZ[p].astype(F32)
    BY[...] = total.reshape(NY, rows, F)
    by = [
        send(BY.at[j], SY.at[j], by_s.at[j], by_r.at[j], dp, at_y(j)) for j in range(1, NY)
    ]

    AF[...] = full(0)
    ggw_v[...] = dot_rows(tokens_all, AF[...]).astype(BF16)
    outs.append(pltpu.make_async_copy(ggw_v, ggw_o, out_sem.at[1]))
    outs[1].start()
    AF[...] = full(1)
    guw_v[...] = dot_rows(tokens_all, AF[...]).astype(BF16)
    outs.append(pltpu.make_async_copy(guw_v, guw_o, out_sem.at[2]))
    outs[2].start()

    outs.append(pltpu.make_async_copy(BZ.at[0], SZ.at[0], out_sem.at[3]))
    outs[3].start()
    outs.append(pltpu.make_async_copy(BY.at[0], SY.at[0], out_sem.at[4]))
    outs[4].start()
    drain(len(sent) - len(by) - len(bz))
    for copy in outs[:2]:
        copy.wait()
    for copy in by + bz:
        copy.wait_recv()
    drain(len(sent))
    for copy in outs[2:]:
        copy.wait()


def closing_kernel(*refs):
    came, sem = refs[10:15], refs[17]
    gone = refs[15:17] + refs[12:15]
    inward = [pltpu.make_async_copy(refs[i], came[i], sem.at[0, i]) for i in range(5)]
    outward = [pltpu.make_async_copy(gone[i], refs[5 + i], sem.at[1, i]) for i in range(5)]
    for copy in inward:
        copy.start()
    for i in range(2):
        inward[i].wait()
        last = came[i][0]
        for j in range(1, came[i].shape[0]):
            last += came[i][j]
        gone[i][...] = last
        outward[i].start()
    for i in range(2, 5):
        inward[i].wait()
        outward[i].start()
    for copy in outward:
        copy.wait()


def solution(mesh):
    dp_n, mp_n = mesh.shape["dp"], mesh.shape["mp"]
    NQ, NY = dp_n // 2, min(4, mp_n // 4)
    NZ = mp_n // NY

    def local(tokens, gate_weight, up_weight, down_weight, cotangent):
        rows, F = tokens.shape
        U = gate_weight.shape[1]
        H = U // 2
        packed = F // LANES * NY * 2 * rows + (2 * rows if F % LANES else 0)
        T = rows * mp_n
        R = T // dp_n
        dma = pltpu.SemaphoreType.DMA
        hbm = pl.BlockSpec(memory_space=pltpu.HBM)
        anywhere = pl.BlockSpec(memory_space=pl.ANY)
        limit = pltpu.CompilerParams(vmem_limit_bytes=60 * 1024 * 1024)
        scratch = [
            ((rows, F), BF16), ((rows, F), BF16),
            ((F, U), BF16), ((F, U), BF16), ((F, U), BF16),
            ((2, F, U), BF16), ((2, F, H), BF16), ((F, U), BF16), ((F, H), BF16),
            ((NY, 2 * rows, F), BF16), ((NZ, packed, LANES), BF16), ((NZ, packed, LANES), BF16),
            ((2, T // 2, F), BF16), ((2, T // 2, F), BF16),
            ((2, NQ, R, 3 * H), BF16), ((2, NQ, R, 3 * H), BF16), ((2, 2, NQ, R, 3 * H), BF16),
            ((2, NY, NZ // 2 * rows, F), BF16), ((2, NY, NZ // 2 * rows, F), BF16),
            ((NZ, NY * rows, F), BF16), ((NZ, NY * rows, F), BF16),
            ((NY, rows, F), F32), ((NZ, rows, F), F32), ((T, U), BF16),
            ((F, U), BF16), ((F, U), BF16), ((F, U), BF16),
        ]
        sems = [(5,), (2,), (2,), (NY,), (NY,), (NZ,), (NZ,), (NZ,), (NZ,), (2, NQ), (2, NQ),
                (2, NQ), (2, NQ), (2, NQ), (2, NQ), (2, NY), (2, NY), (NZ,), (NZ,),
                (NY,), (NY,), (NZ,), (NZ,), (5,)]
        shapes = (
            jax.ShapeDtypeStruct((rows, F), F32), jax.ShapeDtypeStruct((rows, F), F32),
            jax.ShapeDtypeStruct((F, U), BF16), jax.ShapeDtypeStruct((F, U), BF16),
            jax.ShapeDtypeStruct((F, U), BF16),
        )
        terms = (
            jax.ShapeDtypeStruct((NZ, rows, F), F32), jax.ShapeDtypeStruct((NY, rows, F), F32),
        )
        results = pl.pallas_call(
            functools.partial(kernel, (NQ, NZ, NY)),
            out_shape=terms + shapes[2:],
            in_specs=[hbm] * 5,
            out_specs=(anywhere,) * 5,
            scratch_shapes=[pltpu.VMEM(s, t) for s, t in scratch] + [dma(n) for n in sems],
            compiler_params=pltpu.CompilerParams(
                collective_id=0, has_side_effects=True, vmem_limit_bytes=56 * 1024 * 1024
            ),
        )(tokens, cotangent, gate_weight, up_weight, down_weight.T)
        lo, gi, ggw, guw, gdw = pl.pallas_call(
            closing_kernel,
            out_shape=shapes,
            in_specs=[anywhere] * 5,
            out_specs=(anywhere,) * 5,
            scratch_shapes=[pltpu.VMEM(x.shape, x.dtype) for x in terms + shapes[2:] + shapes[:2]]
            + [dma((2, 5))],
            compiler_params=limit,
        )(*results)
        return lo, gi, ggw, guw, gdw.T

    return jax.shard_map(
        local,
        mesh=mesh,
        in_specs=(P("mp", "dp"), P("dp", "mp"), P("dp", "mp"), P("mp", "dp"), P("mp", "dp")),
        out_specs=(P("mp", "dp"), P("mp", "dp"), P("dp", "mp"), P("dp", "mp"), P("mp", "dp")),
        check_vma=False,
    )
```

```python
import functools

import jax
import jax.numpy as jnp
from jax import lax
from jax.experimental import pallas as pl
from jax.experimental.pallas import tpu as pltpu
from jax.sharding import PartitionSpec as P

GELU_SCALE = 0.7978845608028654
CUBIC_TERM = 0.044715
ROWS_DIMS = (((0,), (0,)), ((), ()))
COLS_DIMS = (((1,), (1,)), ((), ()))
MESH_ID = pl.DeviceIdType.MESH
F32 = jnp.float32
BF16 = jnp.bfloat16
LANES = 128


def gelu_parts(values):
    tanh_part = jnp.tanh(GELU_SCALE * (values + CUBIC_TERM * values * values * values))
    gelu_value = 0.5 * values * (1.0 + tanh_part)
    gelu_slope = 0.5 * (1.0 + tanh_part) + 0.5 * values * (
        1.0 - tanh_part * tanh_part
    ) * GELU_SCALE * (1.0 + 3.0 * CUBIC_TERM * values * values)
    return (gelu_value, gelu_slope)


def dot(a, b):
    return jnp.dot(a, b, preferred_element_type=F32)


def dot_cols(a, b):
    return lax.dot_general(a, b, COLS_DIMS, preferred_element_type=F32)


def dot_rows(a, b):
    return lax.dot_general(a, b, ROWS_DIMS, preferred_element_type=F32)


def kernel(
    sizes,
    tok_h, cot_h, gate_h, up_h, down_h,
    SZ, SY, ggw_o, guw_o, gdw_o,
    tok, cot, GV, UV, DV, WF, DF, WS, DS, XY, XZ, XO, XS, TK, CT, PB, RP, HB,
    AY, RY, AZ, RZ, BY, BZ, AF, ggw_v, guw_v, gdw_v,
    ld_sem, wx_s, wx_r, py_s, py_r, pz_s, pz_r, yz_s, yz_r, xs_s, xs_r, rs_s, rs_r,
    ag_s, ag_r, fw_s, fw_r, ay_s, ay_r, az_s, az_r, by_s, by_r, bz_s, bz_r, out_sem,
):
    NQ, NZ, NY = sizes
    order = [0]
    for first in (2, 1):
        order += sorted(range(first, NZ, 2), key=lambda k: -min(k, NZ - k))
    slots = NZ // 2
    rows = tok.shape[0]
    F, H = DF.shape[1], DF.shape[2]
    part_rows = slots * NY * rows
    R = PB.shape[2]
    dp = lax.axis_index("dp")
    mp = lax.axis_index("mp")
    c = lax.rem(dp, 2)
    oc = 1 - c
    q = lax.div(dp, 2)
    sib = dp + 1 - 2 * c
    z = lax.div(mp, NY)
    y = lax.rem(mp, NY)

    sent = []

    def send(src, dst, ssem, rsem, to_dp, to_mp):
        copy = pltpu.make_async_remote_copy(
            src_ref=src, dst_ref=dst, send_sem=ssem, recv_sem=rsem,
            device_id=(to_dp, to_mp), device_id_type=MESH_ID,
        )
        copy.start()
        sent.append(copy)
        return copy

    def drain(n):
        for copy in sent[:n]:
            copy.wait_send()
        del sent[:n]

    NX = NQ // 2
    qx = lax.div(q, 2)
    qy = lax.rem(q, 2)
    steps = [(dx, dy) for dx in range(NX) for dy in range(2)][1:]
    steps.sort(key=lambda s: -min(s[0], NX - s[0]) - s[1])

    def ahead(k):
        dx, dy = steps[k - 1]
        return 2 * lax.rem(qx + dx, NX) + lax.rem(qy + dy, 2)

    def behind(k):
        dx, dy = steps[k - 1]
        return 2 * lax.rem(qx + NX - dx, NX) + lax.rem(qy + dy, 2)

    def peer(k):
        return 2 * ahead(k) + c

    def at_z(k):
        return lax.rem(z + k, NZ) * NY + y

    def at_y(j):
        return z * NY + lax.rem(y + j, NY)

    loads = [
        pltpu.make_async_copy(gate_h, GV, ld_sem.at[0]),
        pltpu.make_async_copy(up_h, UV, ld_sem.at[1]),
        pltpu.make_async_copy(down_h, DV, ld_sem.at[2]),
    ]
    rows_in = [
        pltpu.make_async_copy(tok_h, tok, ld_sem.at[3]),
        pltpu.make_async_copy(cot_h, cot, ld_sem.at[4]),
    ]
    for copy in rows_in:
        copy.start()
    for copy in loads:
        copy.start()

    barrier = pltpu.get_barrier_semaphore()
    partners = [(sib, mp)]
    partners += [(peer(k), mp) for k in range(1, NQ)]
    partners += [(dp, at_z(k)) for k in range(1, NZ)]
    partners += [(dp, at_y(j)) for j in range(1, NY)]
    for partner in partners:
        pl.semaphore_signal(barrier, inc=1, device_id=partner, device_id_type=MESH_ID)
    for copy in rows_in:
        copy.wait()
    XY[0] = jnp.concatenate([tok[...].astype(F32), cot[...].astype(F32)], axis=0).astype(BF16)
    pl.semaphore_wait(barrier, len(partners))

    py = [
        send(XY.at[0], XY.at[j], py_s.at[j], py_r.at[j], dp, at_y(NY - j))
        for j in sorted(range(1, NY), key=lambda j: -min(j, NY - j))
    ]
    pz = [None] * NZ
    for p in range(slots, NZ):
        pz[p] = send(
            XY.at[0], XZ.at[p - slots], pz_s.at[p], pz_r.at[p], dp, at_z(NZ - order[p])
        )
    for copy in loads:
        copy.wait()
    for h in range(2):
        half = slice(h * H, (h + 1) * H)
        WF[h] = jnp.concatenate([GV[:, half], UV[:, half]], axis=1)
        DF[h] = DV[:, half]
    wx = [
        send(WF.at[oc], WS, wx_s.at[0], wx_r.at[0], sib, mp),
        send(DF.at[oc], DS, wx_s.at[1], wx_r.at[1], sib, mp),
    ]
    for copy in py:
        copy.wait_recv()
    lanes = XO.shape[2]
    whole, rest = F // lanes, F % lanes
    block_rows = NY * 2 * rows

    def pack(blocks, at):
        for t in range(whole):
            XO[at, t * block_rows : (t + 1) * block_rows] = blocks[
                :, :, t * lanes : (t + 1) * lanes
            ].reshape(block_rows, lanes)
        if rest:
            XO[at, whole * block_rows :] = jnp.concatenate(
                [blocks[j, :, whole * lanes :] for j in range(NY)], axis=1
            )

    pack(XY, 0)
    for p in range(1, slots):
        pz[p] = send(XO.at[0], XO.at[p], pz_s.at[p], pz_r.at[p], dp, at_z(NZ - order[p]))
    xs = [send(XO.at[0], XS.at[0], xs_s.at[0], xs_r.at[0], sib, mp)]

    def rows_of(ref, m):
        packed = ref[m * slots : (m + 1) * slots].astype(F32)
        both = [packed[:, t * block_rows : (t + 1) * block_rows] for t in range(whole)]
        if rest:
            last = packed[:, whole * block_rows :]
            last = [last[:, :, j * rest : (j + 1) * rest] for j in range(NY)]
            both.append(jnp.stack(last, axis=1).reshape(slots, block_rows, rest))
        both = jnp.concatenate(both, axis=2).reshape(slots * NY, 2, rows, F)
        return (
            both[:, 0].reshape(part_rows, F).astype(BF16),
            both[:, 1].reshape(part_rows, F).astype(BF16),
        )

    for p in range(slots, NZ):
        pz[p].wait_recv()
    pack(XZ, slots)
    for j in range(1, NY):
        p = slots + j
        pz[p] = send(XO.at[slots], XO.at[p], yz_s.at[j], yz_r.at[j], dp, at_y(NY - j))

    rs = []
    for m in range(2):
        for p in range(max(1, m * slots), (m + 1) * slots):
            if p != slots:
                pz[p].wait_recv()
            xs.append(send(XO.at[p], XS.at[p], xs_s.at[p], xs_r.at[p], sib, mp))
        t_own, c_own = rows_of(XO, m)
        TK[m] = t_own
        CT[m] = c_own
        gu = dot(t_own, WF[c])
        gh = dot(c_own, DF[c])
        if m == 0:
            for copy in wx:
                copy.wait_recv()
        for p in range(m * slots, (m + 1) * slots):
            xs[p].wait_recv()
        t_sib, c_sib = rows_of(XS, m)
        gu += dot(t_sib, WS[...])
        PB[m, :, :, 0 : 2 * H] = gu.astype(BF16).reshape(NQ, R, 2 * H)
        gh += dot(c_sib, DS[...])
        PB[m, :, :, 2 * H : 3 * H] = gh.astype(BF16).reshape(NQ, R, H)
        rs.append([
            send(
                PB.at[m, ahead(k)], RP.at[m, q], rs_s.at[m, k], rs_r.at[m, k], peer(k), mp
            )
            for k in range(1, NQ)
        ])
        RP[m, q] = PB[m, q]

    ag = []
    fw = []
    for m in range(2):
        for copy in rs[m]:
            copy.wait_recv()
        sums = RP[m, 0].astype(F32)
        for i in range(1, NQ):
            sums += RP[m, i].astype(F32)
        g_sum, u_sum, gh_sum = sums[:, :H], sums[:, H : 2 * H], sums[:, 2 * H :]
        gelu_value, gelu_slope = gelu_parts(g_sum)
        HB[c, m, q] = jnp.concatenate(
            [gh_sum * u_sum * gelu_slope, gh_sum * gelu_value, gelu_value * u_sum], axis=1
        ).astype(BF16)
        block = HB.at[c, m, q]
        ag.append([
            send(block, block, ag_s.at[m, k], ag_r.at[m, k], peer(k), mp) for k in range(1, NQ)
        ])
        fw.append([send(block, block, fw_s.at[m, 0], fw_r.at[m, 0], sib, mp)])

    az = []
    ay = []
    for m in range(2):
        for k in range(NQ - 1, 0, -1):
            ag[m][k - 1].wait_recv()
            block = HB.at[c, m, behind(k)]
            fw[m].append(send(block, block, fw_s.at[m, k], fw_r.at[m, k], sib, mp))
        acts = HB[c, m].reshape(part_rows, 3 * H)
        lo = dot_cols(acts[:, 2 * H :], DF[c])
        gi = dot_cols(acts[:, : 2 * H], WF[c])
        for copy in fw[m]:
            copy.wait_recv()
        acts = HB[oc, m].reshape(part_rows, 3 * H)
        lo += dot_cols(acts[:, 2 * H :], DF[oc])
        lo = lo.reshape(slots, NY, rows, F)
        for j in range(NY):
            AY[m, j] = (lo[:, j] if m == 0 else lo[j]).reshape(slots * rows, F).astype(BF16)
        for j in range(1, NY):
            ay.append(send(AY.at[m, j], RY.at[m, j], ay_s.at[m, j], ay_r.at[m, j], dp, at_y(j)))
        RY[m, 0] = AY[m, 0]
        gi += dot_cols(acts[:, : 2 * H], WF[oc])
        gi = gi.reshape(slots, NY, rows, F)
        for p in range(slots):
            terms = gi[p] if m == 0 else gi[:, p]
            AZ[m * slots + p] = terms.reshape(NY * rows, F).astype(BF16)
        for p in range(max(1, m * slots), (m + 1) * slots):
            az.append(send(AZ.at[p], RZ.at[p], az_s.at[p], az_r.at[p], dp, at_z(order[p])))
        if m == 0:
            RZ[0] = AZ[0]

    tokens_all = TK[...].reshape(2 * part_rows, F)
    cot_all = CT[...].reshape(2 * part_rows, F)

    def full(i):
        halves = [HB[h, :, :, :, i * H : (i + 1) * H].reshape(2 * part_rows, H) for h in range(2)]
        return jnp.concatenate(halves, axis=1)

    AF[...] = full(2)
    gdw_v[...] = dot_rows(cot_all, AF[...]).astype(BF16)
    outs = [pltpu.make_async_copy(gdw_v, gdw_o, out_sem.at[0])]
    outs[0].start()

    for copy in ay:
        copy.wait_recv()
    total = RY[:, 0].astype(F32)
    for j in range(1, NY):
        total += RY[:, j].astype(F32)
    BZ[...] = total.reshape(NZ, rows, F)
    bz = [
        send(BZ.at[p], SZ.at[p], bz_s.at[p], bz_r.at[p], dp, at_z(order[p])) for p in range(1, NZ)
    ]
    for copy in az:
        copy.wait_recv()
    total = RZ[0].astype(F32)
    for p in range(1, NZ):
        total += RZ[p].astype(F32)
    BY[...] = total.reshape(NY, rows, F)
    by = [
        send(BY.at[j], SY.at[j], by_s.at[j], by_r.at[j], dp, at_y(j)) for j in range(1, NY)
    ]

    AF[...] = full(0)
    ggw_v[...] = dot_rows(tokens_all, AF[...]).astype(BF16)
    outs.append(pltpu.make_async_copy(ggw_v, ggw_o, out_sem.at[1]))
    outs[1].start()
    AF[...] = full(1)
    guw_v[...] = dot_rows(tokens_all, AF[...]).astype(BF16)
    outs.append(pltpu.make_async_copy(guw_v, guw_o, out_sem.at[2]))
    outs[2].start()

    outs.append(pltpu.make_async_copy(BZ.at[0], SZ.at[0], out_sem.at[3]))
    outs[3].start()
    outs.append(pltpu.make_async_copy(BY.at[0], SY.at[0], out_sem.at[4]))
    outs[4].start()
    drain(len(sent) - len(by) - len(bz))
    for copy in outs[:2]:
        copy.wait()
    for copy in by + bz:
        copy.wait_recv()
    drain(len(sent))
    for copy in outs[2:]:
        copy.wait()


def closing_kernel(*refs):
    came, sem = refs[10:15], refs[17]
    gone = refs[15:17] + refs[12:15]
    inward = [pltpu.make_async_copy(refs[i], came[i], sem.at[0, i]) for i in range(5)]
    outward = [pltpu.make_async_copy(gone[i], refs[5 + i], sem.at[1, i]) for i in range(5)]
    for copy in inward:
        copy.start()
    for i in range(2):
        inward[i].wait()
        last = came[i][0]
        for j in range(1, came[i].shape[0]):
            last += came[i][j]
        gone[i][...] = last
        outward[i].start()
    for i in range(2, 5):
        inward[i].wait()
        outward[i].start()
    for copy in outward:
        copy.wait()


def solution(mesh):
    dp_n, mp_n = mesh.shape["dp"], mesh.shape["mp"]
    NQ, NY = dp_n // 2, min(4, mp_n // 4)
    NZ = mp_n // NY

    def local(tokens, gate_weight, up_weight, down_weight, cotangent):
        rows, F = tokens.shape
        U = gate_weight.shape[1]
        H = U // 2
        packed = F // LANES * NY * 2 * rows + (2 * rows if F % LANES else 0)
        T = rows * mp_n
        R = T // dp_n
        dma = pltpu.SemaphoreType.DMA
        hbm = pl.BlockSpec(memory_space=pltpu.HBM)
        anywhere = pl.BlockSpec(memory_space=pl.ANY)
        limit = pltpu.CompilerParams(vmem_limit_bytes=60 * 1024 * 1024)
        scratch = [
            ((rows, F), BF16), ((rows, F), BF16),
            ((F, U), BF16), ((F, U), BF16), ((F, U), BF16),
            ((2, F, U), BF16), ((2, F, H), BF16), ((F, U), BF16), ((F, H), BF16),
            ((NY, 2 * rows, F), BF16), ((NY, 2 * rows, F), BF16), ((NZ, packed, LANES), BF16), ((NZ, packed, LANES), BF16),
            ((2, T // 2, F), BF16), ((2, T // 2, F), BF16),
            ((2, NQ, R, 3 * H), BF16), ((2, NQ, R, 3 * H), BF16), ((2, 2, NQ, R, 3 * H), BF16),
            ((2, NY, NZ // 2 * rows, F), BF16), ((2, NY, NZ // 2 * rows, F), BF16),
            ((NZ, NY * rows, F), BF16), ((NZ, NY * rows, F), BF16),
            ((NY, rows, F), F32), ((NZ, rows, F), F32), ((T, U), BF16),
            ((F, U), BF16), ((F, U), BF16), ((F, U), BF16),
        ]
        sems = [(5,), (2,), (2,), (NY,), (NY,), (NZ,), (NZ,), (NY,), (NY,), (NZ,), (NZ,), (2, NQ), (2, NQ),
                (2, NQ), (2, NQ), (2, NQ), (2, NQ), (2, NY), (2, NY), (NZ,), (NZ,),
                (NY,), (NY,), (NZ,), (NZ,), (5,)]
        shapes = (
            jax.ShapeDtypeStruct((rows, F), F32), jax.ShapeDtypeStruct((rows, F), F32),
            jax.ShapeDtypeStruct((F, U), BF16), jax.ShapeDtypeStruct((F, U), BF16),
            jax.ShapeDtypeStruct((F, U), BF16),
        )
        terms = (
            jax.ShapeDtypeStruct((NZ, rows, F), F32), jax.ShapeDtypeStruct((NY, rows, F), F32),
        )
        results = pl.pallas_call(
            functools.partial(kernel, (NQ, NZ, NY)),
            out_shape=terms + shapes[2:],
            in_specs=[hbm] * 5,
            out_specs=(anywhere,) * 5,
            scratch_shapes=[pltpu.VMEM(s, t) for s, t in scratch] + [dma(n) for n in sems],
            compiler_params=pltpu.CompilerParams(
                collective_id=0, has_side_effects=True, vmem_limit_bytes=56 * 1024 * 1024
            ),
        )(tokens, cotangent, gate_weight, up_weight, down_weight.T)
        lo, gi, ggw, guw, gdw = pl.pallas_call(
            closing_kernel,
            out_shape=shapes,
            in_specs=[anywhere] * 5,
            out_specs=(anywhere,) * 5,
            scratch_shapes=[pltpu.VMEM(x.shape, x.dtype) for x in terms + shapes[2:] + shapes[:2]]
            + [dma((2, 5))],
            compiler_params=limit,
        )(*results)
        return lo, gi, ggw, guw, gdw.T

    return jax.shard_map(
        local,
        mesh=mesh,
        in_specs=(P("mp", "dp"), P("dp", "mp"), P("dp", "mp"), P("mp", "dp"), P("mp", "dp")),
        out_specs=(P("mp", "dp"), P("mp", "dp"), P("dp", "mp"), P("dp", "mp"), P("mp", "dp")),
        check_vma=False,
    )
```
